256 devices in a mesh: tile: 8 (over z), frame: 32 (over y, x, core).
Axes of the slice: x: 4, y: 4, z: 8, core: 2. Of those that a mesh axis runs over, the one named last changes fastest.
Arguments:
- movie: bfloat16 [8, 32, 1024, 5760], P('tile', 'frame'), may hold values from -6 to 6
- frame_shift: int32 [8, 32, 2], P('tile', 'frame'), may hold values from -4 to 4
- intersection: int32 [8], replicated, may hold values from 0 to 512, as said below
- seam_shift: int32 [8], replicated, may hold values from 0 to 127
Outputs:
- micrograph: bfloat16 [8, 1024, 5760], P('tile', 'frame')
- seam_score: float32 [8, 128], P('tile')
The draws below stay inside these ranges and needn't reach their ends.
Inputs may be any that keep to these rules, and one draw needn't show every extreme that they name: intersection[t] is 0 exactly where t % 8 == 8 - 1 (the last tile of a grid row), else between 128 and 512.
All inputs are finite; a program needn't handle non-finite values.
Results may differ from the reference program's by a relative error of at most 0.0048.
Values may be sent and summed in bfloat16 or wider, within the bound.
No kernel may reach another device: no remote copies, remote signals or barrier semaphores. Data moves between devices by JAX's collectives and lax.ppermute only.
A program may use at most 128 MiB of HBM per device.

```python
import math
import jax
import jax.numpy as jnp
from jax import lax

COLS = 5760
SHIFT = 4
STRIP = 512
MINW = 128
LAGS = 128
GRID_W = 8
TILES = 8
FRAMES = 32
ROWS = 1024


def draw_intersection(key, part):
    key = jax.random.fold_in(key, 11)
    widths = jax.random.randint(key, (TILES,), MINW, STRIP + 1)
    places = jnp.arange(TILES)
    widths = jnp.where(places % GRID_W == GRID_W - 1, 0, widths)
    return jnp.where(places == 0, STRIP, widths).astype(jnp.int32)


def touch_ends(values, stream_key, low, top_value):
    extent = values.shape
    index_at = [jax.random.randint(jax.random.fold_in(stream_key, axis), (), 0, extent[axis]) for axis in range(len(extent))]
    values = values.at[tuple(index_at)].set(low)
    longest = extent.index(max(extent))
    index_at[longest] = (index_at[longest] + 1) % extent[longest]
    return values.at[tuple(index_at)].set(top_value)


def levels(stream_key, extent, shards, low, largest):
    def one(position, parts):
        steps = jax.random.uniform(jax.random.fold_in(jax.random.fold_in(stream_key, 6), position), (parts,), jnp.float32, low / len(shards), largest / len(shards))
        return jnp.repeat(jnp.exp(steps), extent[position] // parts).reshape((-1,) + (1,) * (len(extent) - position - 1))

    loudness = one(*shards[0])
    for cut in shards[1:]:
        loudness = loudness * one(*cut)
    return loudness


def centred(stream_key, dims, width, limit, shards=(), kind=jnp.bfloat16):
    result = jax.random.normal(stream_key, dims, jnp.float32) * width
    if len(shards) > 0:
        result = levels(stream_key, dims, shards, -0.22, 0.18) * result
    return jnp.clip(result, min=-limit, max=limit).astype(kind)


def setup_inputs(seed: int = 0) -> dict:
    streams_of = jax.random.split(jax.random.key(seed), 5)
    return {
        "movie": centred(streams_of[0], (TILES, FRAMES, ROWS, COLS), 1.0, 6.0, ((0, 8), (1, 32))),
        "frame_shift": touch_ends(jax.random.randint(streams_of[1], (TILES, FRAMES, 2), 0 - SHIFT, SHIFT + 1), jax.random.fold_in(streams_of[1], 1), 0 - SHIFT, SHIFT).astype(jnp.int32),
        "intersection": draw_intersection(jax.random.fold_in(streams_of[4], 71), 0),
        "seam_shift": touch_ends(jax.random.randint(streams_of[3], (TILES,), 0, LAGS), jax.random.fold_in(streams_of[3], 1), 0, LAGS - 1).astype(jnp.int32),
    }


def right_seam(own_right, next_left, seam_width, shift_now):
    strip_cols = own_right.shape[1]
    lag_count = next_left.shape[1] - strip_cols
    padded = jnp.pad(next_left, ((0, 0), (strip_cols, 0)))
    aligned = lax.dynamic_slice_in_dim(padded, seam_width, strip_cols + lag_count, 1)
    column = jnp.arange(strip_cols, dtype=jnp.int32)
    inside = column >= strip_cols - seam_width
    masked = jnp.where(inside[None, :], own_right, jnp.zeros_like(own_right))
    lag_index = column[None, :] + jnp.arange(lag_count, dtype=jnp.int32)[:, None]
    hankel = aligned[:, lag_index]
    products = jnp.einsum('yk,ylk->l', masked.astype(jnp.float32), hankel.astype(jnp.float32))
    shifted = lax.dynamic_slice_in_dim(padded, seam_width + shift_now, strip_cols, 1).astype(jnp.float32)
    feather = ((strip_cols - column).astype(jnp.float32) - 0.5) / jnp.maximum(seam_width, 1).astype(jnp.float32)
    own_value = own_right.astype(jnp.float32)
    blended = jnp.where(inside[None, :], feather[None, :] * own_value + (1.0 - feather[None, :]) * shifted, own_value)
    return (products, blended)

def left_seam(own_left, prev_right, width_left, shift_left):
    strip_cols = prev_right.shape[1]
    lag_count = own_left.shape[1] - strip_cols
    padded = jnp.pad(prev_right, ((0, 0), (lag_count, strip_cols + lag_count)))
    previous = lax.dynamic_slice_in_dim(padded, lag_count + strip_cols - width_left - shift_left, strip_cols + lag_count, 1).astype(jnp.float32)
    column = jnp.arange(strip_cols + lag_count, dtype=jnp.int32)
    inside = (column >= shift_left) & (column < shift_left + width_left)
    feather = ((width_left - column + shift_left).astype(jnp.float32) - 0.5) / jnp.maximum(width_left, 1).astype(jnp.float32)
    own_value = own_left.astype(jnp.float32)
    return jnp.where(inside[None, :], feather[None, :] * previous + (1.0 - feather[None, :]) * own_value, own_value)

def reference(movie, frame_shift, intersection, seam_shift):
    scale = 1.0 / math.sqrt(FRAMES)

    def sum_tile(pieces):
        frames, moves = pieces

        def add_frame(running, element):
            one_frame, frame_move = element
            padded = jnp.pad(one_frame.astype(jnp.float32), ((SHIFT, SHIFT), (SHIFT, SHIFT)))
            moved = lax.dynamic_slice(padded, (SHIFT - frame_move[0], SHIFT - frame_move[1]), (ROWS, COLS))
            return (running + moved, None)
        running, _ = lax.scan(add_frame, jnp.zeros((ROWS, COLS), jnp.float32), (frames, moves))
        return (running * scale).astype(jnp.bfloat16)
    summed = lax.map(sum_tile, (movie, frame_shift))
    next_left = jnp.concatenate([summed[1:, :, :STRIP + LAGS], jnp.zeros((1, ROWS, STRIP + LAGS), jnp.bfloat16)], 0)
    prev_right = jnp.concatenate([jnp.zeros((1, ROWS, STRIP), jnp.bfloat16), summed[:-1, :, COLS - STRIP:]], 0)
    widths_left = jnp.concatenate([jnp.zeros((1,), jnp.int32), intersection[:-1]])
    shifts_left = jnp.concatenate([jnp.zeros((1,), jnp.int32), seam_shift[:-1]])

    def finish(pieces):
        image, next_piece, prev_piece, seam_width, shift_now, width_left, shift_left = pieces
        products, right_part = right_seam(image[:, COLS - STRIP:], next_piece, seam_width, shift_now)
        left_part = left_seam(image[:, :STRIP + LAGS], prev_piece, width_left, shift_left)
        middle = image[:, STRIP + LAGS:COLS - STRIP]
        tile_image = jnp.concatenate([left_part.astype(jnp.bfloat16), middle, right_part.astype(jnp.bfloat16)], 1)
        score = products / jnp.sqrt((ROWS * jnp.maximum(seam_width, 1)).astype(jnp.float32))
        return (tile_image, score)
    micrograph, seam_score = lax.map(finish, (summed, next_left, prev_right, intersection, seam_shift, widths_left, shifts_left))
    return (micrograph, seam_score)
```

```python
import functools
import math

import jax
import jax.numpy as jnp
from jax import lax
from jax.experimental import pallas as pl
from jax.experimental.pallas import tpu as pltpu
from jax.sharding import PartitionSpec as P

SHIFT = 4
STRIP = 512
LAGS = 128
LANES = 128
EDGE = STRIP + LAGS
SIDE = 4
BAND = 32
HALO = 16
WINDOW = 2 * BAND + 2 * HALO
PAD = 8
VMEM = 48 * 1024 * 1024


def device_at(y, x, core):
    return (y * SIDE + x) * 2 + core


def moved_by(array, y=0, x=0, core=0):
    pairs = [
        (device_at(i, j, k), device_at((i + y) % SIDE, (j + x) % SIDE, (k + core) % 2))
        for i in range(SIDE)
        for j in range(SIDE)
        for k in range(2)
    ]
    return lax.ppermute(array, "frame", pairs)


def from_behind(array, axis, by):
    count = lax.axis_size(axis)
    pairs = [(i, i + by) for i in range(count) if 0 <= i + by < count]
    return lax.ppermute(array, axis, pairs)


def window_start(step, rows):
    return jnp.clip(2 * BAND * step - HALO, 0, rows - WINDOW)


def shift_kernel(pieces, cols, rows, meta, *refs):
    count = len(pieces)
    sources, outs, scratch = refs[:count], refs[count : count + 2], refs[count + 2 :]
    step = pl.program_id(0)
    core, down, right = meta[2], meta[3], meta[4]
    inside = 2 * BAND * step - window_start(step, rows)
    over = jnp.where(right < 0, 1, 0)
    turn = jnp.where(right < 0, LANES + right, right)
    lane = lax.broadcasted_iota(jnp.int32, (BAND, LANES), 1)
    place = 0
    for (first, width), source, held in zip(pieces, sources, scratch):
        low = 0 if first > 0 else 1

        @pl.when(step == 0)
        def _():
            held[...] = jnp.zeros_like(held)

        for k in range(source.shape[1] // LANES):
            held[low + k, PAD : PAD + WINDOW, :] = source[
                :, k * LANES : (k + 1) * LANES
            ].astype(jnp.float32)
        for which, out in ((core, outs[0]), (1 - core, outs[1])):
            top = PAD + inside + BAND * which - down
            before = None
            for k in range(width // LANES + 1):
                now = pltpu.roll(held[k + over, pl.ds(top, BAND), :], turn, 1)
                if k > 0:
                    value = jnp.where(lane < turn, before, now)
                    begin = place + (k - 1) * LANES
                    out[0, 0, :, begin : begin + LANES] = value.astype(jnp.bfloat16)
                before = now
        place += width


def shifted(frame, meta, pieces, x_first):
    rows, cols = frame.shape
    total = sum(width for _, width in pieces)
    in_specs, scratch = [], []
    for first, width in pieces:
        begin = max(first - LANES, 0)
        end = min(first + width + LANES, cols)
        in_specs.append(
            pl.BlockSpec(
                (pl.Element(WINDOW), pl.Element(end - begin)),
                functools.partial(
                    lambda start, i, m: (pl.multiple_of(window_start(i, rows), HALO), start), begin
                ),
            )
        )
        scratch.append(pltpu.VMEM((width // LANES + 2, WINDOW + 2 * PAD, LANES), jnp.float32))

    def place(i, m):
        by_y = lax.rem(i // SIDE - m[0] + SIDE, SIDE)
        by_x = lax.rem(lax.rem(i, SIDE) - m[1] + SIDE, SIDE)
        return (by_x, by_y, 0, 0) if x_first else (by_y, by_x, 0, 0)

    out_spec = pl.BlockSpec((1, 1, BAND, total), place)
    out = jax.ShapeDtypeStruct((SIDE, SIDE, BAND, total), jnp.bfloat16)
    return pl.pallas_call(
        functools.partial(shift_kernel, pieces, cols, rows),
        grid_spec=pltpu.PrefetchScalarGridSpec(
            num_scalar_prefetch=1,
            grid=(SIDE * SIDE,),
            in_specs=in_specs,
            out_specs=[out_spec, out_spec],
            scratch_shapes=scratch,
        ),
        out_shape=[out, out],
        compiler_params=pltpu.CompilerParams(vmem_limit_bytes=VMEM),
        cost_estimate=pl.CostEstimate(
            flops=4 * rows * total, bytes_accessed=5 * rows * total, transcendentals=0
        ),
    )(meta, *[frame] * len(pieces))


def wide(array):
    return array.astype(jnp.float32)


def ahead(array, axis, by):
    return moved_by(array, x=by) if axis == "x" else moved_by(array, y=by)


def reduced(mine, theirs, axes):
    other = moved_by(theirs, core=1)

    def pair(j):
        return wide(mine[j]) + wide(other[j])

    first = [ahead(pair(j).astype(jnp.bfloat16), axes[0], j) for j in (1, 3, 2)]

    def row(j):
        return (wide(mine[0, j]) + wide(other[0, j])) + (
            (wide(first[0][j]) + wide(first[1][j])) + wide(first[2][j])
        )

    second = [ahead(row(j).astype(jnp.bfloat16), axes[1], j) for j in (1, 3, 2)]
    return row(0) + ((wide(second[0]) + wide(second[1])) + wide(second[2]))


def seam_kernel(meta, own_left, own_right, next_left, prev_right, left_out, right_out, score_out):
    width_now, shift_now, width_left, shift_left = meta[0], meta[1], meta[2], meta[3]
    rows = own_left.shape[0]
    mine = own_right[...].astype(jnp.float32)
    after = next_left[...].astype(jnp.float32)
    column = lax.broadcasted_iota(jnp.int32, (rows, STRIP), 1)
    inside = column >= STRIP - width_now
    aligned = pltpu.roll(after, lax.rem(STRIP - width_now - shift_now + EDGE, EDGE), 1)[:, :STRIP]
    feather = ((STRIP - column).astype(jnp.float32) - 0.5) / jnp.maximum(width_now, 1).astype(
        jnp.float32
    )
    right_out[...] = jnp.where(inside, feather * mine + (1.0 - feather) * aligned, mine).astype(
        right_out.dtype
    )
    own = own_left[...].astype(jnp.float32)
    before = jnp.concatenate(
        [prev_right[...].astype(jnp.float32), jnp.zeros((rows, LAGS), jnp.float32)], 1
    )
    before = pltpu.roll(before, lax.rem(shift_left + width_left - STRIP + EDGE, EDGE), 1)
    place = lax.broadcasted_iota(jnp.int32, (rows, EDGE), 1)
    within = (place >= shift_left) & (place < shift_left + width_left)
    weight = ((width_left - place + shift_left).astype(jnp.float32) - 0.5) / jnp.maximum(
        width_left, 1
    ).astype(jnp.float32)
    left_out[...] = jnp.where(within, weight * before + (1.0 - weight) * own, own).astype(
        left_out.dtype
    )
    masked = jnp.where(inside, mine, 0.0)
    masked = pltpu.roll(masked, lax.rem(width_now, STRIP), 1).astype(jnp.bfloat16)
    after = next_left[...]
    gram = jnp.zeros((LANES, 2 * LANES), jnp.float32)
    for t in range(STRIP // LANES):
        gram += lax.dot_general(
            masked[:, t * LANES : (t + 1) * LANES],
            after[:, t * LANES : (t + 2) * LANES],
            (((0,), (0,)), ((), ())),
            preferred_element_type=jnp.float32,
        )
    line = lax.broadcasted_iota(jnp.int32, gram.shape, 0)
    step = 1
    while step < LANES:
        gram = jnp.where((line & step) != 0, pltpu.roll(gram, 2 * LANES - step, 1), gram)
        step *= 2
    scale = lax.rsqrt(
        jnp.full((8, LANES), 1, jnp.int32).astype(jnp.float32)
        * (meta[4] * jnp.maximum(width_now, 1)).astype(jnp.float32)
    )
    total = jnp.sum(gram[:, :LANES], axis=0, keepdims=True)
    score_out[...] = jnp.broadcast_to(total, (8, LANES)) * scale


def seams(meta, own_left, own_right, next_left, prev_right):
    rows = own_left.shape[0]
    return pl.pallas_call(
        seam_kernel,
        in_specs=[pl.BlockSpec(memory_space=pltpu.SMEM)]
        + [pl.BlockSpec(memory_space=pltpu.VMEM)] * 4,
        out_specs=[pl.BlockSpec(memory_space=pltpu.VMEM)] * 3,
        out_shape=[
            jax.ShapeDtypeStruct((rows, EDGE), jnp.bfloat16),
            jax.ShapeDtypeStruct((rows, STRIP), jnp.bfloat16),
            jax.ShapeDtypeStruct((8, LANES), jnp.float32),
        ],
        cost_estimate=pl.CostEstimate(
            flops=2 * rows * STRIP * 2 * LANES, bytes_accessed=10 * rows * EDGE, transcendentals=0
        ),
    )(meta, own_left, own_right, next_left, prev_right)


FIRST_TILES = 14


def body(movie, frame_shift, intersection, seam_shift):
    frame = movie[0, 0]
    rows, cols = frame.shape
    frames = lax.axis_size("frame")
    position = lax.axis_index("frame")
    tile = lax.axis_index("tile")
    y, x, core = position // (2 * SIDE), (position // 2) % SIDE, position % 2
    meta = jnp.concatenate([jnp.stack([y, x, core]).astype(jnp.int32), frame_shift[0, 0]])

    cut = EDGE + FIRST_TILES * LANES
    strips = [(0, EDGE), (cols - STRIP, STRIP)]
    parts = [
        (strips, ("x", "y")),
        ([(cut, cols - STRIP - cut)], ("y", "x")),
        ([(EDGE, cut - EDGE)], ("x", "y")),
    ]
    scale = 1.0 / math.sqrt(frames)
    sums = []
    for pieces, axes in parts:
        mine, theirs = shifted(frame, meta, pieces, axes[0] == "x")
        sums.append((reduced(mine, theirs, axes) * scale).astype(jnp.bfloat16))
    strip, middle_b, middle_a = sums
    own_left, own_right = strip[:, :EDGE], strip[:, EDGE:]

    next_left = from_behind(own_left, "tile", -1)
    prev_right = from_behind(own_right, "tile", 1)
    earlier = jnp.maximum(tile - 1, 0)
    seam_meta = jnp.stack(
        [
            intersection[tile],
            seam_shift[tile],
            jnp.where(tile > 0, intersection[earlier], 0),
            jnp.where(tile > 0, seam_shift[earlier], 0),
            jnp.int32(rows),
        ]
    )
    left_part, right_part, products = seams(seam_meta, own_left, own_right, next_left, prev_right)
    spread_out = jnp.broadcast_to(products[None, :1], (frames, 1, LAGS))
    score = jnp.sum(lax.all_to_all(spread_out, "frame", 0, 0), axis=0)
    image = jnp.concatenate([left_part, middle_a, middle_b, right_part], 1)
    return (image[None], score)


def solution(mesh):
    placed = (P("tile", "frame", None, None), P("tile", "frame", None), P(), P())
    return jax.shard_map(
        body,
        mesh=mesh,
        in_specs=placed,
        out_specs=(P("tile", "frame", None), P("tile", None)),
        check_vma=False,
    )
```

```python
import functools
import math

import jax
import jax.numpy as jnp
from jax import lax
from jax.experimental import pallas as pl
from jax.experimental.pallas import tpu as pltpu
from jax.sharding import PartitionSpec as P

STRIP = 512
LAGS = 128
LANES = 128
EDGE = STRIP + LAGS
SIDE = 4
BAND = 32
HALO = 16
PAD = 8
VMEM = 16 * 1024 * 1024
GATE = 1024 * 1024
LOADING = 36 * 1024 * 1024


def device_at(y, x, core):
    return (y * SIDE + x) * 2 + core


def permuted(array, target):
    places = [(y, x, core) for y in range(SIDE) for x in range(SIDE) for core in range(2)]
    return lax.ppermute(
        array, "frame", [(device_at(*place), device_at(*target(*place))) for place in places]
    )


def to_other_core(array):
    return permuted(array, lambda y, x, core: (y, x, 1 - core))


def ahead(array, stage, by):
    def target(y, x, core):
        if (core == 0) == (stage == 1):
            return (y, (x + by) % SIDE, core)
        return ((y + by) % SIDE, x, core)

    return permuted(array, target)


def from_behind(array, axis, by):
    count = lax.axis_size(axis)
    pairs = [(i, i + by) for i in range(count) if 0 <= i + by < count]
    return lax.ppermute(array, axis, pairs)


def wide(array):
    return array.astype(jnp.float32)


def call(kernel, out_shape, operands, scalars=(), after=(), scratch=()):
    vmem = pl.BlockSpec(memory_space=pltpu.VMEM)
    anywhere = pl.BlockSpec(memory_space=pl.ANY)
    first, last = len(scalars) + len(operands), len(scalars) + len(operands) + len(after)

    def run(*refs):
        kernel(*refs[:first], *refs[last:])

    return pl.pallas_call(
        run,
        in_specs=[pl.BlockSpec(memory_space=pltpu.SMEM)] * len(scalars)
        + [vmem] * len(operands)
        + [anywhere] * len(after),
        out_specs=[vmem] * len(out_shape),
        out_shape=[jax.ShapeDtypeStruct(shape, dtype) for shape, dtype in out_shape],
        scratch_shapes=list(scratch),
        compiler_params=pltpu.CompilerParams(vmem_limit_bytes=VMEM),
        cost_estimate=pl.CostEstimate(flops=1024, bytes_accessed=1024, transcendentals=0),
    )(*scalars, *operands, *after)


def gated(arrays, after):
    anywhere = pl.BlockSpec(memory_space=pl.ANY)
    return pl.pallas_call(
        lambda *refs: None,
        in_specs=[anywhere] * (len(arrays) + len(after)),
        out_specs=[anywhere] * len(arrays),
        out_shape=[jax.ShapeDtypeStruct(array.shape, array.dtype) for array in arrays],
        input_output_aliases={i: i for i in range(len(arrays))},
        compiler_params=pltpu.CompilerParams(vmem_limit_bytes=GATE),
        cost_estimate=pl.CostEstimate(flops=1024, bytes_accessed=1024, transcendentals=0),
    )(*arrays, *after)


class Mover:
    def __init__(self, moves, pieces, rows, cols, held, theirs):
        position = lax.axis_index("frame")
        self.y, self.x = position // (2 * SIDE), (position // 2) % SIDE
        core = position % 2
        self.core = 1 - core if theirs else core
        self.down, right = moves[0], moves[1]
        self.over = jnp.where(right < 0, 1, 0)
        self.turn = jnp.where(right < 0, LANES + right, right)
        self.rows, self.held, self.pieces = rows, held, []
        base = 0
        for source, origin, first, width in pieces:
            begin, end = max(first - LANES, 0), min(first + width + LANES, cols)
            blank = jnp.zeros(held.shape[2:], held.dtype)
            for slot in range(2):
                if begin == first:
                    held[slot, base] = blank
                if end == first + width:
                    held[slot, base + width // LANES + 1] = blank
            low = base + (1 if begin == first else 0)
            self.pieces.append((source, begin - origin, (end - begin) // LANES, base, low, width))
            base += width // LANES + 2

    def band(self, slot, j, d, write):
        by_x = jnp.where(self.core == 0, j, d)
        by_y = jnp.where(self.core == 0, d, j)
        chip = lax.rem(self.y + by_y, SIDE) * SIDE + lax.rem(self.x + by_x, SIDE)
        top = pl.multiple_of((chip * 2 + self.core) * BAND, BAND)
        above = pl.multiple_of(jnp.maximum(top - HALO, 0), HALO)
        below = pl.multiple_of(jnp.minimum(top + BAND, self.rows - HALO), HALO)
        has_above = jnp.where(top > 0, 1.0, 0.0).astype(jnp.float32)
        has_below = jnp.where(top + BAND < self.rows, 1.0, 0.0).astype(jnp.float32)
        lane = lax.broadcasted_iota(jnp.int32, (BAND, LANES), 1)
        held, out = self.held, 0
        for source, begin, tiles, base, low, width in self.pieces:
            for k in range(tiles):
                at = pl.ds(begin + k * LANES, LANES)
                held[slot, low + k, :PAD] = wide(source[pl.ds(above, HALO), at])[PAD:] * has_above
                held[slot, low + k, PAD : PAD + BAND] = wide(source[pl.ds(top, BAND), at])
                held[slot, low + k, PAD + BAND :] = (
                    wide(source[pl.ds(below, HALO), at])[:PAD] * has_below
                )
            before = None
            for k in range(width // LANES + 1):
                value = held[slot, base + k + self.over, pl.ds(PAD - self.down, BAND), :]
                now = pltpu.roll(value, self.turn, 1)
                if k > 0:
                    write(out, jnp.where(lane < self.turn, before, now))
                    out += LANES
                before = now


def held_for(widths):
    tiles = sum(width // LANES + 2 for width in widths)
    return pltpu.VMEM((2, tiles, BAND + 2 * PAD, LANES), jnp.float32)


def each_band(mover, count, where, write):
    @pl.loop(0, count // 2)
    def _(pair):
        for slot in range(2):
            n = 2 * pair + slot
            j, d = where(n)
            mover.band(slot, j, d, functools.partial(write, n))


def forward(n):
    return 1 + n // 2, n


def backward(n):
    return 2 + n // 2, n


def own(n):
    return 0, n


def both_ways(n):
    return jnp.where(n < 4, forward(n)[0], backward(n - 4)[0]), lax.rem(n, SIDE)


def later(n):
    return jnp.where(n < 2, 1, jnp.where(n < 4, 3, 0)), lax.rem(jnp.where(n < 4, n + 2, n), SIDE)


def every(n):
    return n // SIDE, lax.rem(n, SIDE)


class Columns:
    def __init__(self, moves, rows, cols, arrays, places):
        self.moves, self.rows, self.cols, self.arrays, self.places = moves, rows, cols, arrays, places
        self.total = sum(width for _, _, width in places)
        self.scratch = [held_for([width for _, _, width in places])]

    def mover(self, moves, sources, held, theirs):
        pieces = [(source, *place) for source, place in zip(sources, self.places)]
        return Mover(moves, pieces, self.rows, self.cols, held, theirs)

    def run(self, body, out_shape, operands, after=(), theirs=False):
        count = len(self.arrays)

        def kernel(moves, *refs):
            mover = self.mover(moves, [refs[0]] * len(self.places), refs[-1], theirs)
            body(mover, *refs[count:-1])

        return call(
            kernel,
            out_shape,
            [*self.arrays, *operands],
            [self.moves],
            after,
            self.scratch,
        )

    def theirs(self, count, where, after=()):
        def body(mover, out):
            def write(n, begin, value):
                out[n, :, begin : begin + LANES] = value.astype(jnp.bfloat16)

            each_band(mover, count, where, write)

        shape = ((count, BAND, self.total), jnp.bfloat16)
        return self.run(body, [shape], [], after, True)[0]

    def loaded(self, frame, parts):
        def kernel(moves, frame, out, bands, held, sems):
            copies = [
                pltpu.make_async_copy(
                    frame.at[:, begin:end], out.at[:, begin:end], sems.at[p]
                )
                for p, (begin, end) in enumerate(parts)
            ]
            for copy in copies:
                copy.start()
            mover = self.mover(moves, [out] * len(self.places), held, True)
            for copy in copies[:-1]:
                copy.wait()

            def write(n, begin, value):
                bands[n, :, begin : begin + LANES] = value.astype(jnp.bfloat16)

            each_band(mover, SIDE * SIDE, every, write)
            copies[-1].wait()

        vmem = pl.BlockSpec(memory_space=pltpu.VMEM)
        return pl.pallas_call(
            kernel,
            in_specs=[
                pl.BlockSpec(memory_space=pltpu.SMEM),
                pl.BlockSpec(memory_space=pltpu.HBM),
            ],
            out_specs=[vmem, vmem],
            out_shape=[
                jax.ShapeDtypeStruct(frame.shape, frame.dtype),
                jax.ShapeDtypeStruct((SIDE * SIDE, BAND, self.total), jnp.bfloat16),
            ],
            scratch_shapes=[*self.scratch, pltpu.SemaphoreType.DMA((len(parts),))],
            compiler_params=pltpu.CompilerParams(vmem_limit_bytes=LOADING),
            cost_estimate=pl.CostEstimate(flops=1024, bytes_accessed=1024, transcendentals=0),
        )(self.moves, frame)

    def pairs(self, other, after=()):
        def body(mover, other, *outs):
            for way, where in enumerate((forward, backward)):

                def write(n, begin, value, way=way):
                    at = slice(begin, begin + LANES)
                    value = value + wide(other[way * SIDE + n, :, at])
                    outs[way][n, :, at] = value.astype(jnp.bfloat16)

                each_band(mover, SIDE, where, write)

        shape = ((SIDE, BAND, self.total), jnp.bfloat16)
        return self.run(body, [shape, shape], [other], after)

    def every_pair(self, other, after=()):
        def body(mover, other, *outs):
            for j in range(SIDE):

                def write(n, begin, value, j=j):
                    at = slice(begin, begin + LANES)
                    value = value + wide(other[j * SIDE + n, :, at])
                    outs[j][n, :, at] = value.astype(outs[j].dtype)

                each_band(mover, SIDE, lambda n, j=j: (j, n), write)

        quarter = (SIDE, BAND, self.total)
        shapes = [(quarter, jnp.float32)] + [(quarter, jnp.bfloat16)] * (SIDE - 1)
        return self.run(body, shapes, [other], after)

    def passed(self, forth, other, got, after=()):
        first, j, d0 = (0, 1, 2) if forth else (2, 3, 0)

        def body(mover, other, got, out):
            def write(n, begin, value):
                at = slice(begin, begin + LANES)
                value = (value + wide(other[first + n, :, at])) + wide(got[d0 + n, :, at])
                out[n, :, at] = value.astype(jnp.bfloat16)

            each_band(mover, 2, lambda n: (j, d0 + n), write)

        shape = ((2, BAND, self.total), jnp.bfloat16)
        return self.run(body, [shape], [other, got], after)[0]

    def rows_of_chip(self, other, forth, back, forth_far, back_far, scores, after=()):
        total = self.total

        def body(mover, other, forth, back, forth_far, back_far, *refs):
            score_refs, outs = refs[:SIDE], refs[SIDE:]
            for n in range(SIDE):
                near = forth if n < 2 else back
                far = back_far if n < 2 else forth_far

                def write(begin, value, n=n, near=near, far=far):
                    at = slice(begin, begin + LANES)
                    value = value + wide(other[SIDE + n, :, at])
                    value = value + (wide(near[n, :, at]) + wide(far[n % 2, :, at]))
                    outs[n][:, at] = value.astype(outs[n].dtype)

                mover.band(n % 2, 0, n, write)
            score = (score_refs[0][...] + score_refs[1][...]) + (
                score_refs[2][...] + score_refs[3][...]
            )
            high = wide(score.astype(jnp.bfloat16))
            middle = wide((score - high).astype(jnp.bfloat16))
            low = (score - high) - middle
            line = lax.broadcasted_iota(jnp.int32, score.shape, 0)
            three = jnp.where(line == 0, high, jnp.where(line == 1, middle, low))
            three = jnp.where(line < 3, three, 0.0)
            three = jnp.concatenate([three, jnp.zeros((BAND - PAD, LANES), jnp.float32)], 0)
            for out in outs:
                out[:, total:] = three.astype(out.dtype)

        wider = (BAND, total + LANES)
        shapes = [(wider, jnp.float32)] + [(wider, jnp.bfloat16)] * (SIDE - 1)
        operands = [other, forth, back, forth_far, back_far, *scores]
        return self.run(body, shapes, operands, after)


def row_kernel(mine, a, b, c, *outs):
    for d in range(SIDE):
        value = mine[d] + ((wide(a[d]) + wide(b[d])) + wide(c[d]))
        outs[d][...] = value.astype(outs[d].dtype)


def edge_kernel(scale, mine, a, b, c, left, right, right_sent):
    value = mine[...] + ((wide(a[...]) + wide(b[...])) + wide(c[...]))
    value = value * scale
    left[...] = value[:, :EDGE]
    right[...] = value[:, EDGE:]
    right_sent[...] = value[:, EDGE:].astype(jnp.bfloat16)


def image_kernel(scale, left, right, mine, a, b, c, out, score):
    total = mine.shape[1] - LANES
    out[:, :EDGE] = left[...]
    for begin in range(0, total, LANES):
        at = slice(begin, begin + LANES)
        value = mine[:, at] + ((wide(a[:, at]) + wide(b[:, at])) + wide(c[:, at]))
        out[:, EDGE + begin : EDGE + begin + LANES] = (value * scale).astype(jnp.bfloat16)
    out[:, EDGE + total :] = right[...]
    at = slice(total, total + LANES)
    value = mine[:PAD, at] + ((wide(a[:, at]) + wide(b[:, at])) + wide(c[:, at]))[:PAD]
    score[...] = jnp.sum(value, axis=0, keepdims=True)


def seam_kernel(
    widths, shifts, all_rows, own_left, own_right, next_left, prev_right, left_out, right_out, score_out
):
    tile = lax.axis_index("tile")
    earlier = jnp.maximum(tile - 1, 0)
    width_now, shift_now = widths[tile], shifts[tile]
    width_left = jnp.where(tile > 0, widths[earlier], 0)
    shift_left = jnp.where(tile > 0, shifts[earlier], 0)
    rows = own_left.shape[0]

    def rounded(ref):
        return wide(ref[...].astype(jnp.bfloat16))

    mine, after = rounded(own_right), rounded(next_left)
    column = lax.broadcasted_iota(jnp.int32, (rows, STRIP), 1)
    inside = column >= STRIP - width_now
    aligned = pltpu.roll(after, lax.rem(STRIP - width_now - shift_now + EDGE, EDGE), 1)[:, :STRIP]
    feather = ((STRIP - column).astype(jnp.float32) - 0.5) / jnp.maximum(width_now, 1).astype(
        jnp.float32
    )
    right_out[...] = jnp.where(inside, feather * mine + (1.0 - feather) * aligned, mine).astype(
        right_out.dtype
    )
    mine = rounded(own_left)
    before = jnp.concatenate(
        [prev_right[...].astype(jnp.float32), jnp.zeros((rows, LAGS), jnp.float32)], 1
    )
    before = pltpu.roll(before, lax.rem(shift_left + width_left - STRIP + EDGE, EDGE), 1)
    place = lax.broadcasted_iota(jnp.int32, (rows, EDGE), 1)
    within = (place >= shift_left) & (place < shift_left + width_left)
    weight = ((width_left - place + shift_left).astype(jnp.float32) - 0.5) / jnp.maximum(
        width_left, 1
    ).astype(jnp.float32)
    left_out[...] = jnp.where(within, weight * before + (1.0 - weight) * mine, mine).astype(
        left_out.dtype
    )
    masked = jnp.where(inside, own_right[...], 0.0)
    masked = pltpu.roll(masked, lax.rem(width_now, STRIP), 1)
    after = next_left[...]
    mine_high, after_high = masked.astype(jnp.bfloat16), after.astype(jnp.bfloat16)
    mine_low = (masked - wide(mine_high)).astype(jnp.bfloat16)
    after_low = (after - wide(after_high)).astype(jnp.bfloat16)
    gram = jnp.zeros((LANES, 2 * LANES), jnp.float32)
    for t in range(STRIP // LANES):
        for one, two in ((mine_high, after_high), (mine_high, after_low), (mine_low, after_high)):
            gram += lax.dot_general(
                one[:, t * LANES : (t + 1) * LANES],
                two[:, t * LANES : (t + 2) * LANES],
                (((0,), (0,)), ((), ())),
                preferred_element_type=jnp.float32,
            )
    line = lax.broadcasted_iota(jnp.int32, gram.shape, 0)
    step = 1
    while step < LANES:
        gram = jnp.where((line & step) != 0, pltpu.roll(gram, 2 * LANES - step, 1), gram)
        step *= 2
    total = jnp.sum(gram[:, :LANES], axis=0, keepdims=True)
    terms = jnp.full((PAD, LANES), all_rows * jnp.maximum(width_now, 1), jnp.int32)
    score_out[...] = jnp.broadcast_to(total, (PAD, LANES)) / jnp.sqrt(terms.astype(jnp.float32))


def body(movie, frame_shift, intersection, seam_shift):
    frame = movie[0, 0]
    rows, cols = frame.shape
    scale = 1.0 / math.sqrt(lax.axis_size("frame"))
    moves = frame_shift[0, 0]

    low, high = EDGE + LANES, cols - STRIP - LANES
    places = [(0, 0, EDGE), (0, cols - STRIP, STRIP)]
    frame, theirs_s = Columns(moves, rows, cols, [], places).loaded(
        frame, [(0, low), (high, cols), (low, high)]
    )
    strips = Columns(moves, rows, cols, [frame], places)
    middle = Columns(moves, rows, cols, [frame], [(0, EDGE, cols - STRIP - EDGE)])

    other_s = to_other_core(theirs_s)
    theirs_m = middle.theirs(2 * SIDE, both_ways, [theirs_s])
    other_m = to_other_core(*gated([theirs_m], [other_s]))
    pair_s = strips.every_pair(other_s, [theirs_m])
    got_s = [ahead(pair_s[j], 1, j) for j in (1, 2, 3)]
    theirs_l = middle.theirs(2 * SIDE, later, [pair_s[0]])
    other_l = to_other_core(theirs_l)
    pair_m = middle.pairs(other_m, [theirs_l])
    pair_f, pair_b = gated(pair_m, got_s)
    got_f, got_b = ahead(pair_f, 1, 1), ahead(pair_b, 1, -1)

    band = (BAND, EDGE + STRIP)
    row_s = call(
        row_kernel,
        [(band, jnp.float32)] + [(band, jnp.bfloat16)] * (SIDE - 1),
        [pair_s[0], *got_s],
        after=[pair_f, other_l],
    )
    own_left, own_right, sent_right = call(
        functools.partial(edge_kernel, scale),
        [((BAND, EDGE), jnp.float32), ((BAND, STRIP), jnp.float32), ((BAND, STRIP), jnp.bfloat16)],
        [row_s[0], *[ahead(row_s[j], 2, j) for j in (1, 2, 3)]],
    )
    next_left = from_behind(own_left, "tile", -1)
    prev_right = from_behind(sent_right, "tile", 1)
    left_part, right_part, score = call(
        lambda widths, shifts, *refs: seam_kernel(widths, shifts, rows, *refs),
        [((BAND, EDGE), jnp.bfloat16), ((BAND, STRIP), jnp.bfloat16), ((PAD, LANES), jnp.float32)],
        [own_left, own_right, next_left, prev_right],
        [intersection, seam_shift],
    )
    far_f = ahead(middle.passed(True, other_l, got_f, [score]), 1, 1)
    far_b = ahead(middle.passed(False, other_l, got_b, [score]), 1, -1)
    score = score + to_other_core(score)
    scores = [score, *[ahead(score, 1, j) for j in (1, 2, 3)]]
    row_m = middle.rows_of_chip(other_l, got_f, got_b, far_f, far_b, scores)
    image, score = call(
        functools.partial(image_kernel, scale),
        [((BAND, cols), jnp.bfloat16), ((1, LAGS), jnp.float32)],
        [left_part, right_part, row_m[0], *[ahead(row_m[j], 2, j) for j in (1, 2, 3)]],
    )
    return (image[None], score)


def solution(mesh):
    placed = (P("tile", "frame", None, None), P("tile", "frame", None), P(), P())
    return jax.shard_map(
        body,
        mesh=mesh,
        in_specs=placed,
        out_specs=(P("tile", "frame", None), P("tile", None)),
        check_vma=False,
    )
```

```python
import functools
import math

import jax
import jax.numpy as jnp
from jax import lax
from jax.experimental import pallas as pl
from jax.experimental.pallas import tpu as pltpu
from jax.sharding import PartitionSpec as P

STRIP = 512
LAGS = 128
LANES = 128
EDGE = STRIP + LAGS
SIDE = 4
BAND = 32
HALO = 16
PAD = 8
VMEM = 16 * 1024 * 1024
GATE = 1024 * 1024
LOADING = 36 * 1024 * 1024


def device_at(y, x, core):
    return (y * SIDE + x) * 2 + core


def permuted(array, target):
    places = [(y, x, core) for y in range(SIDE) for x in range(SIDE) for core in range(2)]
    return lax.ppermute(
        array, "frame", [(device_at(*place), device_at(*target(*place))) for place in places]
    )


def to_other_core(array):
    return permuted(array, lambda y, x, core: (y, x, 1 - core))


def ahead(array, stage, by):
    def target(y, x, core):
        if (core == 0) == (stage == 1):
            return (y, (x + by) % SIDE, core)
        return ((y + by) % SIDE, x, core)

    return permuted(array, target)


def direct(arrays, stage):
    return [ahead(arrays[j], stage, j) for j in (2, 1, 3)]


def from_behind(array, axis, by):
    count = lax.axis_size(axis)
    pairs = [(i, i + by) for i in range(count) if 0 <= i + by < count]
    return lax.ppermute(array, axis, pairs)


def wide(array):
    return array.astype(jnp.float32)


def call(kernel, out_shape, operands, scalars=(), after=(), scratch=()):
    vmem = pl.BlockSpec(memory_space=pltpu.VMEM)
    anywhere = pl.BlockSpec(memory_space=pl.ANY)
    first, last = len(scalars) + len(operands), len(scalars) + len(operands) + len(after)

    def run(*refs):
        kernel(*refs[:first], *refs[last:])

    return pl.pallas_call(
        run,
        in_specs=[pl.BlockSpec(memory_space=pltpu.SMEM)] * len(scalars)
        + [vmem] * len(operands)
        + [anywhere] * len(after),
        out_specs=[vmem] * len(out_shape),
        out_shape=[jax.ShapeDtypeStruct(shape, dtype) for shape, dtype in out_shape],
        scratch_shapes=list(scratch),
        compiler_params=pltpu.CompilerParams(vmem_limit_bytes=VMEM),
        cost_estimate=pl.CostEstimate(flops=1024, bytes_accessed=1024, transcendentals=0),
    )(*scalars, *operands, *after)


def gated(arrays, after):
    anywhere = pl.BlockSpec(memory_space=pl.ANY)
    return pl.pallas_call(
        lambda *refs: None,
        in_specs=[anywhere] * (len(arrays) + len(after)),
        out_specs=[anywhere] * len(arrays),
        out_shape=[jax.ShapeDtypeStruct(array.shape, array.dtype) for array in arrays],
        input_output_aliases={i: i for i in range(len(arrays))},
        compiler_params=pltpu.CompilerParams(vmem_limit_bytes=GATE),
        cost_estimate=pl.CostEstimate(flops=1024, bytes_accessed=1024, transcendentals=0),
    )(*arrays, *after)


class Mover:
    def __init__(self, moves, pieces, rows, cols, held, theirs):
        position = lax.axis_index("frame")
        self.y, self.x = position // (2 * SIDE), (position // 2) % SIDE
        core = position % 2
        self.core = 1 - core if theirs else core
        self.down, right = moves[0], moves[1]
        self.over = jnp.where(right < 0, 1, 0)
        self.turn = jnp.where(right < 0, LANES + right, right)
        self.rows, self.held, self.pieces = rows, held, []
        base = 0
        for source, origin, first, width in pieces:
            begin, end = max(first - LANES, 0), min(first + width + LANES, cols)
            blank = jnp.zeros(held.shape[2:], held.dtype)
            for slot in range(2):
                if begin == first:
                    held[slot, base] = blank
                if end == first + width:
                    held[slot, base + width // LANES + 1] = blank
            low = base + (1 if begin == first else 0)
            self.pieces.append((source, begin - origin, (end - begin) // LANES, base, low, width))
            base += width // LANES + 2

    def band(self, slot, j, d, write):
        by_x = jnp.where(self.core == 0, j, d)
        by_y = jnp.where(self.core == 0, d, j)
        chip = lax.rem(self.y + by_y, SIDE) * SIDE + lax.rem(self.x + by_x, SIDE)
        top = pl.multiple_of((chip * 2 + self.core) * BAND, BAND)
        above = pl.multiple_of(jnp.maximum(top - HALO, 0), HALO)
        below = pl.multiple_of(jnp.minimum(top + BAND, self.rows - HALO), HALO)
        has_above = jnp.where(top > 0, 1.0, 0.0).astype(jnp.float32)
        has_below = jnp.where(top + BAND < self.rows, 1.0, 0.0).astype(jnp.float32)
        lane = lax.broadcasted_iota(jnp.int32, (BAND, LANES), 1)
        held, out = self.held, 0
        for source, begin, tiles, base, low, width in self.pieces:
            for k in range(tiles):
                at = pl.ds(begin + k * LANES, LANES)
                held[slot, low + k, :PAD] = wide(source[pl.ds(above, HALO), at])[PAD:] * has_above
                held[slot, low + k, PAD : PAD + BAND] = wide(source[pl.ds(top, BAND), at])
                held[slot, low + k, PAD + BAND :] = (
                    wide(source[pl.ds(below, HALO), at])[:PAD] * has_below
                )
            before = None
            for k in range(width // LANES + 1):
                value = held[slot, base + k + self.over, pl.ds(PAD - self.down, BAND), :]
                now = pltpu.roll(value, self.turn, 1)
                if k > 0:
                    write(out, jnp.where(lane < self.turn, before, now))
                    out += LANES
                before = now


def held_for(widths):
    tiles = sum(width // LANES + 2 for width in widths)
    return pltpu.VMEM((2, tiles, BAND + 2 * PAD, LANES), jnp.float32)


def each_band(mover, count, where, write):
    @pl.loop(0, count // 2)
    def _(pair):
        for slot in range(2):
            n = 2 * pair + slot
            j, d = where(n)
            mover.band(slot, j, d, functools.partial(write, n))


def forward(n):
    return 1 + n // 2, n


def backward(n):
    return 2 + n // 2, n


def own(n):
    return 0, n


def both_ways(n):
    return jnp.where(n < 4, forward(n)[0], backward(n - 4)[0]), lax.rem(n, SIDE)


def passing(n):
    return jnp.where(n < 2, 1, 3), lax.rem(n + 2, SIDE)


def later(n):
    return jnp.where(n < 4, passing(n)[0], 0), lax.rem(jnp.where(n < 4, n + 2, n), SIDE)


def every(n):
    return n // SIDE, lax.rem(n, SIDE)


class Columns:
    def __init__(self, moves, rows, cols, arrays, places):
        self.moves, self.rows, self.cols, self.arrays, self.places = moves, rows, cols, arrays, places
        self.total = sum(width for _, _, width in places)
        self.scratch = [held_for([width for _, _, width in places])]

    def mover(self, moves, sources, held, theirs):
        pieces = [(source, *place) for source, place in zip(sources, self.places)]
        return Mover(moves, pieces, self.rows, self.cols, held, theirs)

    def run(self, body, out_shape, operands, after=(), theirs=False):
        count = len(self.arrays)

        def kernel(moves, *refs):
            mover = self.mover(moves, [refs[0]] * len(self.places), refs[-1], theirs)
            body(mover, *refs[count:-1])

        return call(
            kernel,
            out_shape,
            [*self.arrays, *operands],
            [self.moves],
            after,
            self.scratch,
        )

    def theirs(self, count, where, after=()):
        def body(mover, out):
            def write(n, begin, value):
                out[n, :, begin : begin + LANES] = value.astype(jnp.bfloat16)

            each_band(mover, count, where, write)

        shape = ((count, BAND, self.total), jnp.bfloat16)
        return self.run(body, [shape], [], after, True)[0]

    def loaded(self, frame, low, high, middle):
        rows, cols = frame.shape
        first, last = middle[0][0], middle[-1][1]
        ends = [min(end + LANES, high) for _, end in middle]
        parts = [(0, low), (high, cols), *zip([low, *ends[:-1]], ends)]
        halves = [slice(i * rows // SIDE, (i + 1) * rows // SIDE) for i in range(SIDE)]

        def kernel(moves_far, frame, out, bands, both, held, held_middle, moves, sems, moves_sem):
            copies = [
                [
                    pltpu.make_async_copy(
                        frame.at[half, begin:end], out.at[half, begin:end], sems.at[p, h]
                    )
                    for h, half in enumerate(halves)
                ]
                for p, (begin, end) in enumerate(parts)
            ]
            moves_copy = pltpu.make_async_copy(moves_far, moves, moves_sem)
            moves_copy.start()
            for pair in copies:
                for copy in pair:
                    copy.start()
            moves_copy.wait()
            for copy in (*copies[0], *copies[1]):
                copy.wait()
            mover = self.mover(moves, [out] * len(self.places), held, True)

            def write(n, begin, value):
                bands[n, :, begin : begin + LANES] = value.astype(jnp.bfloat16)

            each_band(mover, SIDE * SIDE, every, write)
            for pair, (begin, end) in zip(copies[2:], middle):
                for copy in pair:
                    copy.wait()
                mover = Mover(moves, [(out, 0, begin, end - begin)], rows, cols, held_middle, True)

                def write_middle(n, at, value, begin=begin):
                    at = at + begin - first
                    both[n, :, at : at + LANES] = value.astype(jnp.bfloat16)

                each_band(mover, 2 * SIDE, both_ways, write_middle)

        vmem = pl.BlockSpec(memory_space=pltpu.VMEM)
        far = pl.BlockSpec(memory_space=pltpu.HBM)
        widest = max(end - begin for begin, end in middle)
        return pl.pallas_call(
            kernel,
            in_specs=[far, far],
            out_specs=[vmem, vmem, vmem],
            out_shape=[
                jax.ShapeDtypeStruct(frame.shape, frame.dtype),
                jax.ShapeDtypeStruct((SIDE * SIDE, BAND, self.total), jnp.bfloat16),
                jax.ShapeDtypeStruct((2 * SIDE, BAND, last - first), jnp.bfloat16),
            ],
            scratch_shapes=[
                *self.scratch,
                held_for([widest]),
                pltpu.SMEM(self.moves.shape, jnp.int32),
                pltpu.SemaphoreType.DMA((len(parts), len(halves))),
                pltpu.SemaphoreType.DMA,
            ],
            compiler_params=pltpu.CompilerParams(vmem_limit_bytes=LOADING),
            cost_estimate=pl.CostEstimate(flops=1024, bytes_accessed=1024, transcendentals=0),
        )(self.moves, frame)

    def pairs(self, other, after=()):
        def body(mover, other, *outs):
            for way, where in enumerate((forward, backward)):

                def write(n, begin, value, way=way):
                    at = slice(begin, begin + LANES)
                    value = value + wide(other[way * SIDE + n, :, at])
                    outs[way][n, :, at] = value.astype(jnp.bfloat16)

                each_band(mover, SIDE, where, write)

        shape = ((SIDE, BAND, self.total), jnp.bfloat16)
        return self.run(body, [shape, shape], [other], after)

    def every_pair(self, other, after=()):
        def body(mover, other, *outs):
            for j in range(SIDE):

                def write(n, begin, value, j=j):
                    at = slice(begin, begin + LANES)
                    value = value + wide(other[j * SIDE + n, :, at])
                    outs[j][n, :, at] = value.astype(outs[j].dtype)

                each_band(mover, SIDE, lambda n, j=j: (j, n), write)

        quarter = (SIDE, BAND, self.total)
        shapes = [(quarter, jnp.float32)] + [(quarter, jnp.bfloat16)] * (SIDE - 1)
        return self.run(body, shapes, [other], after)

    def later_pairs(self, other, after=()):
        def body(mover, other, *outs):
            for part, out in enumerate(outs):

                def write(n, begin, value, part=part, out=out):
                    at = slice(begin, begin + LANES)
                    out[n, :, at] = value + wide(other[part * SIDE + n, :, at])

                where = (passing, own)[part]
                each_band(mover, SIDE, where, write)

        shape = ((SIDE, BAND, self.total), jnp.float32)
        return self.run(body, [shape, shape], [other], after)


def pass_kernel(first, d0, pair, got, out):
    for n in range(SIDE // 2):
        out[n] = (pair[first + n] + wide(got[d0 + n])).astype(out.dtype)


def passed(forth, pair, got, after=()):
    _, band, total = pair.shape
    return call(
        functools.partial(pass_kernel, *((0, 2) if forth else (2, 0))),
        [((SIDE // 2, band, total), jnp.bfloat16)],
        [pair, got],
        after=after,
    )[0]


def chip_kernel(pair, forth, back, forth_far, back_far, *refs):
    score_refs, outs = refs[:SIDE], refs[SIDE:]
    total = pair.shape[2]
    for n in range(SIDE):
        near = forth if n < 2 else back
        far = back_far if n < 2 else forth_far
        value = pair[n] + (wide(near[n]) + wide(far[n % 2]))
        outs[n][:, :total] = value.astype(outs[n].dtype)
    score = (score_refs[0][...] + score_refs[1][...]) + (score_refs[2][...] + score_refs[3][...])
    high = wide(score.astype(jnp.bfloat16))
    middle = wide((score - high).astype(jnp.bfloat16))
    low = (score - high) - middle
    line = lax.broadcasted_iota(jnp.int32, score.shape, 0)
    three = jnp.where(line == 0, high, jnp.where(line == 1, middle, low))
    three = jnp.where(line < 3, three, 0.0)
    three = jnp.concatenate([three, jnp.zeros((BAND - PAD, LANES), jnp.float32)], 0)
    for out in outs:
        out[:, total:] = three.astype(out.dtype)


def row_kernel(mine, a, b, c, *outs):
    for d in range(SIDE):
        value = mine[d] + ((wide(a[d]) + wide(b[d])) + wide(c[d]))
        outs[d][...] = value.astype(outs[d].dtype)


def edge_kernel(scale, mine, a, b, c, left, right, right_sent):
    value = mine[...] + ((wide(a[...]) + wide(b[...])) + wide(c[...]))
    value = value * scale
    left[...] = value[:, :EDGE]
    right[...] = value[:, EDGE:]
    right_sent[...] = value[:, EDGE:].astype(jnp.bfloat16)


def rounded(ref):
    return wide(ref[...].astype(jnp.bfloat16))


def right_blend(width, shift, own_right, next_left):
    mine, after = rounded(own_right), rounded(next_left)
    column = lax.broadcasted_iota(jnp.int32, mine.shape, 1)
    aligned = pltpu.roll(after, lax.rem(STRIP - width - shift + EDGE, EDGE), 1)[:, :STRIP]
    feather = (wide(STRIP - column) - 0.5) / wide(jnp.maximum(width, 1))
    blend = feather * mine + (1.0 - feather) * aligned
    return jnp.where(column >= STRIP - width, blend, mine)


def left_blend(width, shift, own_left, prev_right):
    mine = rounded(own_left)
    rows = mine.shape[0]
    before = jnp.concatenate([rounded(prev_right), jnp.zeros((rows, LAGS), jnp.float32)], 1)
    before = pltpu.roll(before, lax.rem(shift + width - STRIP + EDGE, EDGE), 1)
    column = lax.broadcasted_iota(jnp.int32, mine.shape, 1)
    feather = (wide(width - column + shift) - 0.5) / wide(jnp.maximum(width, 1))
    blend = feather * before + (1.0 - feather) * mine
    return jnp.where((column >= shift) & (column < shift + width), blend, mine)


def image_kernel(
    scale, widths, shifts, own_left, own_right, next_left, prev_right, mine, a, b, c, out, score
):
    tile = lax.axis_index("tile")
    earlier = jnp.maximum(tile - 1, 0)
    total = mine.shape[1] - LANES
    for begin in range(0, total, LANES):
        at = slice(begin, begin + LANES)
        value = mine[:, at] + ((wide(a[:, at]) + wide(b[:, at])) + wide(c[:, at]))
        out[:, EDGE + begin : EDGE + begin + LANES] = (value * scale).astype(jnp.bfloat16)
    value = right_blend(widths[tile], shifts[tile], own_right, next_left)
    out[:, EDGE + total :] = value.astype(jnp.bfloat16)
    width, shift = jnp.where(tile > 0, widths[earlier], 0), jnp.where(tile > 0, shifts[earlier], 0)
    out[:, :EDGE] = left_blend(width, shift, own_left, prev_right).astype(jnp.bfloat16)
    at = slice(total, total + LANES)
    value = mine[:PAD, at] + ((wide(a[:, at]) + wide(b[:, at])) + wide(c[:, at]))[:PAD]
    score[...] = jnp.sum(value, axis=0, keepdims=True)


def score_kernel(all_rows, widths, own_right, next_left, score_out):
    width = widths[lax.axis_index("tile")]
    column = lax.broadcasted_iota(jnp.int32, own_right.shape, 1)
    masked = jnp.where(column >= STRIP - width, own_right[...], 0.0)
    masked = pltpu.roll(masked, lax.rem(width, STRIP), 1)
    after = next_left[...]
    mine_high, after_high = masked.astype(jnp.bfloat16), after.astype(jnp.bfloat16)
    mine_low = (masked - wide(mine_high)).astype(jnp.bfloat16)
    after_low = (after - wide(after_high)).astype(jnp.bfloat16)
    gram = jnp.zeros((LANES, 2 * LANES), jnp.float32)
    for t in range(STRIP // LANES):
        for one, two in ((mine_high, after_high), (mine_high, after_low), (mine_low, after_high)):
            gram += lax.dot_general(
                one[:, t * LANES : (t + 1) * LANES],
                two[:, t * LANES : (t + 2) * LANES],
                (((0,), (0,)), ((), ())),
                preferred_element_type=jnp.float32,
            )
    line = lax.broadcasted_iota(jnp.int32, gram.shape, 0)
    step = 1
    while step < LANES:
        gram = jnp.where((line & step) != 0, pltpu.roll(gram, 2 * LANES - step, 1), gram)
        step *= 2
    total = jnp.sum(gram[:, :LANES], axis=0, keepdims=True)
    terms = jnp.full((PAD, LANES), all_rows * jnp.maximum(width, 1), jnp.int32)
    score_out[...] = jnp.broadcast_to(total, (PAD, LANES)) / jnp.sqrt(terms.astype(jnp.float32))


def body(movie, frame_shift, intersection, seam_shift):
    frame = movie[0, 0]
    rows, cols = frame.shape
    scale = 1.0 / math.sqrt(lax.axis_size("frame"))
    moves = frame_shift[0, 0]

    low, high = EDGE + LANES, cols - STRIP - LANES
    places = [(0, 0, EDGE), (0, cols - STRIP, STRIP)]
    third = (cols - STRIP - EDGE) // 3 // LANES * LANES
    cuts = [EDGE, EDGE + third, EDGE + 2 * third, cols - STRIP]
    frame, theirs_s, theirs_m = Columns(moves, rows, cols, [], places).loaded(
        frame, low, high, list(zip(cuts[:-1], cuts[1:]))
    )
    strips = Columns(moves, rows, cols, [frame], places)
    middle = Columns(moves, rows, cols, [frame], [(0, EDGE, cols - STRIP - EDGE)])

    other_s = to_other_core(theirs_s)
    theirs_l = middle.theirs(2 * SIDE, later, [theirs_s])
    other_m = to_other_core(*gated([theirs_m], [other_s, theirs_l]))
    other_l = to_other_core(theirs_l)
    pair_s = strips.every_pair(other_s, [theirs_l])
    got_s = direct(pair_s, 1)
    pair_m = middle.pairs(other_m, [pair_s[0]])
    pair_f, pair_b = gated(pair_m, got_s)
    got_f, got_b = ahead(pair_f, 1, 1), ahead(pair_b, 1, -1)

    band = (BAND, EDGE + STRIP)
    row_s = call(
        row_kernel,
        [(band, jnp.float32)] + [(band, jnp.bfloat16)] * (SIDE - 1),
        [pair_s[0], *got_s],
        after=[pair_f, other_l],
    )
    own_left, own_right, sent_right = call(
        functools.partial(edge_kernel, scale),
        [((BAND, EDGE), jnp.float32), ((BAND, STRIP), jnp.float32), ((BAND, STRIP), jnp.bfloat16)],
        [row_s[0], *direct(row_s, 2)],
    )
    next_left = from_behind(own_left, "tile", -1)
    prev_right = from_behind(sent_right, "tile", 1)
    passing_m, own_m = middle.later_pairs(other_l, [own_left])
    (score,) = call(
        functools.partial(score_kernel, rows),
        [((PAD, LANES), jnp.float32)],
        [own_right, next_left],
        [intersection],
        after=[passing_m],
    )

    far_f = ahead(passed(True, passing_m, got_f, [score]), 1, 1)
    far_b = ahead(passed(False, passing_m, got_b, [score]), 1, -1)
    score = score + to_other_core(score)
    wider = (BAND, middle.total + LANES)
    row_m = call(
        chip_kernel,
        [(wider, jnp.float32)] + [(wider, jnp.bfloat16)] * (SIDE - 1),
        [own_m, got_f, got_b, far_f, far_b, *[score], *direct([score] * SIDE, 1)],
    )
    image, score = call(
        functools.partial(image_kernel, scale),
        [((BAND, cols), jnp.bfloat16), ((1, LAGS), jnp.float32)],
        [own_left, own_right, next_left, prev_right, row_m[0], *direct(row_m, 2)],
        [intersection, seam_shift],
    )
    return (image[None], score)


def solution(mesh):
    placed = (P("tile", "frame", None, None), P("tile", "frame", None), P(), P())
    return jax.shard_map(
        body,
        mesh=mesh,
        in_specs=placed,
        out_specs=(P("tile", "frame", None), P("tile", None)),
        check_vma=False,
    )
```

```python
import functools
import math

import jax
import jax.numpy as jnp
from jax import lax
from jax.experimental import pallas as pl
from jax.experimental.pallas import tpu as pltpu
from jax.sharding import PartitionSpec as P

STRIP = 512
LAGS = 128
LANES = 128
EDGE = STRIP + LAGS
SIDE = 4
BAND = 32
HALO = 16
PAD = 8
VMEM = 16 * 1024 * 1024
GATE = 1024 * 1024
LOADING = 36 * 1024 * 1024


def device_at(y, x, core):
    return (y * SIDE + x) * 2 + core


def permuted(array, target):
    places = [(y, x, core) for y in range(SIDE) for x in range(SIDE) for core in range(2)]
    return lax.ppermute(
        array, "frame", [(device_at(*place), device_at(*target(*place))) for place in places]
    )


def to_other_core(array):
    return permuted(array, lambda y, x, core: (y, x, 1 - core))


def ahead(array, stage, by):
    def target(y, x, core):
        if (core == 0) == (stage == 1):
            return (y, (x + by) % SIDE, core)
        return ((y + by) % SIDE, x, core)

    return permuted(array, target)


def direct(arrays, stage):
    return [ahead(arrays[j], stage, j) for j in (2, 1, 3)]


def from_behind(array, axis, by):
    count = lax.axis_size(axis)
    pairs = [(i, i + by) for i in range(count) if 0 <= i + by < count]
    return lax.ppermute(array, axis, pairs)


def wide(array):
    return array.astype(jnp.float32)


def call(kernel, out_shape, operands, scalars=(), after=(), scratch=()):
    vmem = pl.BlockSpec(memory_space=pltpu.VMEM)
    anywhere = pl.BlockSpec(memory_space=pl.ANY)
    first, last = len(scalars) + len(operands), len(scalars) + len(operands) + len(after)

    def run(*refs):
        kernel(*refs[:first], *refs[last:])

    return pl.pallas_call(
        run,
        in_specs=[pl.BlockSpec(memory_space=pltpu.SMEM)] * len(scalars)
        + [vmem] * len(operands)
        + [anywhere] * len(after),
        out_specs=[vmem] * len(out_shape),
        out_shape=[jax.ShapeDtypeStruct(shape, dtype) for shape, dtype in out_shape],
        scratch_shapes=list(scratch),
        compiler_params=pltpu.CompilerParams(vmem_limit_bytes=VMEM),
        cost_estimate=pl.CostEstimate(flops=1024, bytes_accessed=1024, transcendentals=0),
    )(*scalars, *operands, *after)


def gated(arrays, after):
    anywhere = pl.BlockSpec(memory_space=pl.ANY)
    return pl.pallas_call(
        lambda *refs: None,
        in_specs=[anywhere] * (len(arrays) + len(after)),
        out_specs=[anywhere] * len(arrays),
        out_shape=[jax.ShapeDtypeStruct(array.shape, array.dtype) for array in arrays],
        input_output_aliases={i: i for i in range(len(arrays))},
        compiler_params=pltpu.CompilerParams(vmem_limit_bytes=GATE),
        cost_estimate=pl.CostEstimate(flops=1024, bytes_accessed=1024, transcendentals=0),
    )(*arrays, *after)


class Mover:
    def __init__(self, moves, pieces, rows, cols, held, theirs):
        position = lax.axis_index("frame")
        self.y, self.x = position // (2 * SIDE), (position // 2) % SIDE
        core = position % 2
        self.core = 1 - core if theirs else core
        self.down, right = moves[0], moves[1]
        self.over = jnp.where(right < 0, 1, 0)
        self.turn = jnp.where(right < 0, LANES + right, right)
        self.rows, self.held, self.pieces = rows, held, []
        base = 0
        for source, origin, first, width in pieces:
            begin, end = max(first - LANES, 0), min(first + width + LANES, cols)
            blank = jnp.zeros(held.shape[2:], held.dtype)
            for slot in range(held.shape[0]):
                if begin == first:
                    held[slot, base] = blank
                if end == first + width:
                    held[slot, base + width // LANES + 1] = blank
            low = base + (1 if begin == first else 0)
            self.pieces.append((source, begin - origin, (end - begin) // LANES, base, low, width))
            base += width // LANES + 2

    def band(self, slot, j, d, write):
        by_x = jnp.where(self.core == 0, j, d)
        by_y = jnp.where(self.core == 0, d, j)
        chip = lax.rem(self.y + by_y, SIDE) * SIDE + lax.rem(self.x + by_x, SIDE)
        top = pl.multiple_of((chip * 2 + self.core) * BAND, BAND)
        above = pl.multiple_of(jnp.maximum(top - HALO, 0), HALO)
        below = pl.multiple_of(jnp.minimum(top + BAND, self.rows - HALO), HALO)
        has_above = jnp.where(top > 0, 1.0, 0.0).astype(jnp.float32)
        has_below = jnp.where(top + BAND < self.rows, 1.0, 0.0).astype(jnp.float32)
        lane = lax.broadcasted_iota(jnp.int32, (BAND, LANES), 1)
        held, out = self.held, 0
        for source, begin, tiles, base, low, width in self.pieces:
            for k in range(tiles):
                at = pl.ds(begin + k * LANES, LANES)
                held[slot, low + k, :PAD] = wide(source[pl.ds(above, HALO), at])[PAD:] * has_above
                held[slot, low + k, PAD : PAD + BAND] = wide(source[pl.ds(top, BAND), at])
                held[slot, low + k, PAD + BAND :] = (
                    wide(source[pl.ds(below, HALO), at])[:PAD] * has_below
                )
            before = None
            for k in range(width // LANES + 1):
                value = held[slot, base + k + self.over, pl.ds(PAD - self.down, BAND), :]
                now = pltpu.roll(value, self.turn, 1)
                if k > 0:
                    write(out, jnp.where(lane < self.turn, before, now))
                    out += LANES
                before = now


def held_for(widths):
    tiles = sum(width // LANES + 2 for width in widths)
    return pltpu.VMEM((2 if tiles > 16 else SIDE, tiles, BAND + 2 * PAD, LANES), jnp.float32)


def each_band(mover, count, where, write):
    slots = mover.held.shape[0]

    @pl.loop(0, count // slots)
    def _(turn):
        for slot in range(slots):
            n = slots * turn + slot
            j, d = where(n)
            mover.band(slot, j, d, functools.partial(write, n))


def forward(n):
    return 1 + n // 2, n


def backward(n):
    return 2 + n // 2, n


def own(n):
    return 0, n


def both_ways(n):
    return jnp.where(n < 4, forward(n)[0], backward(n - 4)[0]), lax.rem(n, SIDE)


def passing(n):
    return jnp.where(n < 2, 1, 3), lax.rem(n + 2, SIDE)


def later(n):
    return jnp.where(n < 4, passing(n)[0], 0), lax.rem(jnp.where(n < 4, n + 2, n), SIDE)


def every(n):
    return n // SIDE, lax.rem(n, SIDE)


class Columns:
    def __init__(self, moves, rows, cols, arrays, places):
        self.moves, self.rows, self.cols, self.arrays, self.places = moves, rows, cols, arrays, places
        self.total = sum(width for _, _, width in places)
        self.scratch = [held_for([width for _, _, width in places])]

    def mover(self, moves, sources, held, theirs):
        pieces = [(source, *place) for source, place in zip(sources, self.places)]
        return Mover(moves, pieces, self.rows, self.cols, held, theirs)

    def run(self, body, out_shape, operands, after=(), theirs=False):
        count = len(self.arrays)

        def kernel(moves, *refs):
            mover = self.mover(moves, [refs[0]] * len(self.places), refs[-1], theirs)
            body(mover, *refs[count:-1])

        return call(
            kernel,
            out_shape,
            [*self.arrays, *operands],
            [self.moves],
            after,
            self.scratch,
        )

    def theirs(self, count, where, after=()):
        def body(mover, out):
            def write(n, begin, value):
                out[n, :, begin : begin + LANES] = value.astype(jnp.bfloat16)

            each_band(mover, count, where, write)

        shape = ((count, BAND, self.total), jnp.bfloat16)
        return self.run(body, [shape], [], after, True)[0]

    def loaded(self, frame, low, high, middle):
        rows, cols = frame.shape
        first, last = middle[0][0], middle[-1][1]
        ends = [min(end + LANES, high) for _, end in middle]
        parts = [(0, low), (high, cols), *zip([low, *ends[:-1]], ends)]
        halves = [slice(i * rows // SIDE, (i + 1) * rows // SIDE) for i in range(SIDE)]

        def kernel(moves_far, frame, out, bands, both, held, held_middle, moves, sems, moves_sem):
            copies = [
                [
                    pltpu.make_async_copy(
                        frame.at[half, begin:end], out.at[half, begin:end], sems.at[p, h]
                    )
                    for h, half in enumerate(halves)
                ]
                for p, (begin, end) in enumerate(parts)
            ]
            moves_copy = pltpu.make_async_copy(moves_far, moves, moves_sem)
            moves_copy.start()
            for pair in copies:
                for copy in pair:
                    copy.start()
            moves_copy.wait()
            for copy in (*copies[0], *copies[1]):
                copy.wait()
            mover = self.mover(moves, [out] * len(self.places), held, True)

            def write(n, begin, value):
                bands[n, :, begin : begin + LANES] = value.astype(jnp.bfloat16)

            each_band(mover, SIDE * SIDE, every, write)
            for pair, (begin, end) in zip(copies[2:], middle):
                for copy in pair:
                    copy.wait()
                mover = Mover(moves, [(out, 0, begin, end - begin)], rows, cols, held_middle, True)

                def write_middle(n, at, value, begin=begin):
                    at = at + begin - first
                    both[n, :, at : at + LANES] = value.astype(jnp.bfloat16)

                each_band(mover, 2 * SIDE, both_ways, write_middle)

        vmem = pl.BlockSpec(memory_space=pltpu.VMEM)
        far = pl.BlockSpec(memory_space=pltpu.HBM)
        widest = max(end - begin for begin, end in middle)
        return pl.pallas_call(
            kernel,
            in_specs=[far, far],
            out_specs=[vmem, vmem, vmem],
            out_shape=[
                jax.ShapeDtypeStruct(frame.shape, frame.dtype),
                jax.ShapeDtypeStruct((SIDE * SIDE, BAND, self.total), jnp.bfloat16),
                jax.ShapeDtypeStruct((2 * SIDE, BAND, last - first), jnp.bfloat16),
            ],
            scratch_shapes=[
                *self.scratch,
                held_for([widest]),
                pltpu.SMEM(self.moves.shape, jnp.int32),
                pltpu.SemaphoreType.DMA((len(parts), len(halves))),
                pltpu.SemaphoreType.DMA,
            ],
            compiler_params=pltpu.CompilerParams(vmem_limit_bytes=LOADING),
            cost_estimate=pl.CostEstimate(flops=1024, bytes_accessed=1024, transcendentals=0),
        )(self.moves, frame)

    def pairs(self, other, after=()):
        def body(mover, other, *outs):
            for way, where in enumerate((forward, backward)):

                def write(n, begin, value, way=way):
                    at = slice(begin, begin + LANES)
                    value = value + wide(other[way * SIDE + n, :, at])
                    outs[way][n, :, at] = value.astype(jnp.bfloat16)

                each_band(mover, SIDE, where, write)

        shape = ((SIDE, BAND, self.total), jnp.bfloat16)
        return self.run(body, [shape, shape], [other], after)

    def every_pair(self, other, after=()):
        def body(mover, other, *outs):
            for j in range(SIDE):

                def write(n, begin, value, j=j):
                    at = slice(begin, begin + LANES)
                    value = value + wide(other[j * SIDE + n, :, at])
                    outs[j][n, :, at] = value.astype(outs[j].dtype)

                each_band(mover, SIDE, lambda n, j=j: (j, n), write)

        quarter = (SIDE, BAND, self.total)
        shapes = [(quarter, jnp.float32)] + [(quarter, jnp.bfloat16)] * (SIDE - 1)
        return self.run(body, shapes, [other], after)

    def later_pairs(self, other, after=()):
        def body(mover, other, *outs):
            for part, out in enumerate(outs):

                def write(n, begin, value, part=part, out=out):
                    at = slice(begin, begin + LANES)
                    out[n, :, at] = value + wide(other[part * SIDE + n, :, at])

                where = (passing, own)[part]
                each_band(mover, SIDE, where, write)

        shape = ((SIDE, BAND, self.total), jnp.float32)
        return self.run(body, [shape, shape], [other], after)


def pass_kernel(pair, forth, back, out_forth, out_back):
    half = SIDE // 2
    for n in range(half):
        out_forth[n] = (pair[n] + wide(forth[half + n])).astype(out_forth.dtype)
        out_back[n] = (pair[half + n] + wide(back[n])).astype(out_back.dtype)


def chip_kernel(pair, forth, back, forth_far, back_far, *refs):
    score_refs, outs = refs[:SIDE], refs[SIDE:]
    total = pair.shape[2]
    for n in range(SIDE):
        near = forth if n < 2 else back
        far = back_far if n < 2 else forth_far
        value = pair[n] + (wide(near[n]) + wide(far[n % 2]))
        outs[n][:, :total] = value.astype(outs[n].dtype)
    score = (score_refs[0][...] + score_refs[1][...]) + (score_refs[2][...] + score_refs[3][...])
    high = wide(score.astype(jnp.bfloat16))
    middle = wide((score - high).astype(jnp.bfloat16))
    low = (score - high) - middle
    line = lax.broadcasted_iota(jnp.int32, score.shape, 0)
    three = jnp.where(line == 0, high, jnp.where(line == 1, middle, low))
    three = jnp.where(line < 3, three, 0.0)
    three = jnp.concatenate([three, jnp.zeros((BAND - PAD, LANES), jnp.float32)], 0)
    for out in outs:
        out[:, total:] = three.astype(out.dtype)


def row_kernel(mine, a, b, c, *outs):
    for d in range(SIDE):
        value = mine[d] + ((wide(a[d]) + wide(b[d])) + wide(c[d]))
        outs[d][...] = value.astype(outs[d].dtype)


def edge_kernel(scale, mine, a, b, c, left, right, right_sent):
    value = mine[...] + ((wide(a[...]) + wide(b[...])) + wide(c[...]))
    value = value * scale
    left[...] = value[:, :EDGE]
    right[...] = value[:, EDGE:]
    right_sent[...] = value[:, EDGE:].astype(jnp.bfloat16)


def rounded(ref):
    return wide(ref[...].astype(jnp.bfloat16))


def right_blend(width, shift, own_right, next_left):
    mine, after = rounded(own_right), rounded(next_left)
    column = lax.broadcasted_iota(jnp.int32, mine.shape, 1)
    aligned = pltpu.roll(after, lax.rem(STRIP - width - shift + EDGE, EDGE), 1)[:, :STRIP]
    feather = (wide(STRIP - column) - 0.5) / wide(jnp.maximum(width, 1))
    blend = feather * mine + (1.0 - feather) * aligned
    return jnp.where(column >= STRIP - width, blend, mine)


def left_blend(width, shift, own_left, prev_right):
    mine = rounded(own_left)
    rows = mine.shape[0]
    before = jnp.concatenate([rounded(prev_right), jnp.zeros((rows, LAGS), jnp.float32)], 1)
    before = pltpu.roll(before, lax.rem(shift + width - STRIP + EDGE, EDGE), 1)
    column = lax.broadcasted_iota(jnp.int32, mine.shape, 1)
    feather = (wide(width - column + shift) - 0.5) / wide(jnp.maximum(width, 1))
    blend = feather * before + (1.0 - feather) * mine
    return jnp.where((column >= shift) & (column < shift + width), blend, mine)


def blend_kernel(widths, shifts, own_left, own_right, next_left, prev_right, left, right):
    tile = lax.axis_index("tile")
    earlier = jnp.maximum(tile - 1, 0)
    value = right_blend(widths[tile], shifts[tile], own_right, next_left)
    right[...] = value.astype(jnp.bfloat16)
    width, shift = jnp.where(tile > 0, widths[earlier], 0), jnp.where(tile > 0, shifts[earlier], 0)
    left[...] = left_blend(width, shift, own_left, prev_right).astype(jnp.bfloat16)


def image_kernel(scale, left, right, mine, a, b, c, out, score):
    total = mine.shape[1] - LANES
    for begin in range(0, total, LANES):
        at = slice(begin, begin + LANES)
        value = mine[:, at] + ((wide(a[:, at]) + wide(b[:, at])) + wide(c[:, at]))
        out[:, EDGE + begin : EDGE + begin + LANES] = (value * scale).astype(jnp.bfloat16)
    out[:, :EDGE] = left[...]
    out[:, EDGE + total :] = right[...]
    at = slice(total, total + LANES)
    value = mine[:PAD, at] + ((wide(a[:, at]) + wide(b[:, at])) + wide(c[:, at]))[:PAD]
    score[...] = jnp.sum(value, axis=0, keepdims=True)


def score_kernel(all_rows, widths, own_right, next_left, score_out):
    width = widths[lax.axis_index("tile")]
    column = lax.broadcasted_iota(jnp.int32, own_right.shape, 1)
    masked = jnp.where(column >= STRIP - width, own_right[...], 0.0)
    masked = pltpu.roll(masked, lax.rem(width, STRIP), 1)
    after = next_left[...]
    mine_high, after_high = masked.astype(jnp.bfloat16), after.astype(jnp.bfloat16)
    mine_low = (masked - wide(mine_high)).astype(jnp.bfloat16)
    after_low = (after - wide(after_high)).astype(jnp.bfloat16)
    pairs = ((mine_high, after_high), (mine_high, after_low), (mine_low, after_high))
    starts = range(0, STRIP, LANES)
    gram = lax.dot_general(
        jnp.concatenate([one[:, t : t + LANES] for one, _ in pairs for t in starts], 0),
        jnp.concatenate([two[:, t : t + 2 * LANES] for _, two in pairs for t in starts], 0),
        (((0,), (0,)), ((), ())),
        preferred_element_type=jnp.float32,
    )
    line = lax.broadcasted_iota(jnp.int32, gram.shape, 0)
    step = 1
    while step < LANES:
        gram = jnp.where((line & step) != 0, pltpu.roll(gram, 2 * LANES - step, 1), gram)
        step *= 2
    total = jnp.sum(gram[:, :LANES], axis=0, keepdims=True)
    terms = jnp.full((PAD, LANES), all_rows * jnp.maximum(width, 1), jnp.int32)
    score_out[...] = jnp.broadcast_to(total, (PAD, LANES)) / jnp.sqrt(terms.astype(jnp.float32))


def body(movie, frame_shift, intersection, seam_shift):
    frame = movie[0, 0]
    rows, cols = frame.shape
    scale = 1.0 / math.sqrt(lax.axis_size("frame"))
    moves = frame_shift[0, 0]

    low, high = EDGE + LANES, cols - STRIP - LANES
    places = [(0, 0, EDGE), (0, cols - STRIP, STRIP)]
    ninth = (cols - STRIP - EDGE) // 9 // LANES * LANES
    cuts = [EDGE, EDGE + 4 * ninth, EDGE + 7 * ninth, cols - STRIP]
    frame, theirs_s, theirs_m = Columns(moves, rows, cols, [], places).loaded(
        frame, low, high, list(zip(cuts[:-1], cuts[1:]))
    )
    strips = Columns(moves, rows, cols, [frame], places)
    middle = Columns(moves, rows, cols, [frame], [(0, EDGE, cols - STRIP - EDGE)])

    other_s = to_other_core(theirs_s)
    theirs_l = middle.theirs(2 * SIDE, later, [theirs_s])
    other_m = to_other_core(*gated([theirs_m], [other_s, theirs_l]))
    other_l = to_other_core(theirs_l)
    pair_s = strips.every_pair(other_s, [theirs_l])
    got_s = direct(pair_s, 1)
    pair_m = middle.pairs(other_m, [pair_s[0]])
    pair_f, pair_b = gated(pair_m, got_s)
    got_f, got_b = ahead(pair_f, 1, 1), ahead(pair_b, 1, -1)

    band = (BAND, EDGE + STRIP)
    row_s = call(
        row_kernel,
        [(band, jnp.float32)] + [(band, jnp.bfloat16)] * (SIDE - 1),
        [pair_s[0], *got_s],
        after=[pair_f, other_l],
    )
    own_left, own_right, sent_right = call(
        functools.partial(edge_kernel, scale),
        [((BAND, EDGE), jnp.float32), ((BAND, STRIP), jnp.float32), ((BAND, STRIP), jnp.bfloat16)],
        [row_s[0], *direct(row_s, 2)],
    )
    next_left = from_behind(own_left, "tile", -1)
    prev_right = from_behind(sent_right, "tile", 1)
    passing_m, own_m = middle.later_pairs(other_l, [own_left])
    (score,) = call(
        functools.partial(score_kernel, rows),
        [((PAD, LANES), jnp.float32)],
        [own_right, next_left],
        [intersection],
        after=[passing_m],
    )

    half = (SIDE // 2, BAND, middle.total)
    far_f, far_b = call(
        pass_kernel,
        [(half, jnp.bfloat16)] * 2,
        [passing_m, got_f, got_b],
        after=[score],
    )
    far_f, far_b = ahead(far_f, 1, 1), ahead(far_b, 1, -1)
    score = score + to_other_core(score)
    wider = (BAND, middle.total + LANES)
    row_m = call(
        chip_kernel,
        [(wider, jnp.float32)] + [(wider, jnp.bfloat16)] * (SIDE - 1),
        [own_m, got_f, got_b, far_f, far_b, *[score], *direct([score] * SIDE, 1)],
    )
    left_part, right_part = call(
        blend_kernel,
        [((BAND, EDGE), jnp.bfloat16), ((BAND, STRIP), jnp.bfloat16)],
        [own_left, own_right, next_left, prev_right],
        [intersection, seam_shift],
    )
    image, score = call(
        functools.partial(image_kernel, scale),
        [((BAND, cols), jnp.bfloat16), ((1, LAGS), jnp.float32)],
        [left_part, right_part, row_m[0], *direct(row_m, 2)],
    )
    return (image[None], score)


def solution(mesh):
    placed = (P("tile", "frame", None, None), P("tile", "frame", None), P(), P())
    return jax.shard_map(
        body,
        mesh=mesh,
        in_specs=placed,
        out_specs=(P("tile", "frame", None), P("tile", None)),
        check_vma=False,
    )
```

```python
import functools
import math

import jax
import jax.numpy as jnp
from jax import lax
from jax.experimental import pallas as pl
from jax.experimental.pallas import tpu as pltpu
from jax.sharding import PartitionSpec as P

STRIP = 512
LAGS = 128
LANES = 128
EDGE = STRIP + LAGS
SIDE = 4
BAND = 32
HALO = 16
PAD = 8
VMEM = 16 * 1024 * 1024
GATE = 1024 * 1024
LOADING = 36 * 1024 * 1024


def device_at(y, x, core):
    return (y * SIDE + x) * 2 + core


def permuted(array, target):
    places = [(y, x, core) for y in range(SIDE) for x in range(SIDE) for core in range(2)]
    return lax.ppermute(
        array, "frame", [(device_at(*place), device_at(*target(*place))) for place in places]
    )


def to_other_core(array):
    return permuted(array, lambda y, x, core: (y, x, 1 - core))


def ahead(array, stage, by):
    def target(y, x, core):
        if (core == 0) == (stage == 1):
            return (y, (x + by) % SIDE, core)
        return ((y + by) % SIDE, x, core)

    return permuted(array, target)


def direct(arrays, stage):
    return [ahead(arrays[j], stage, j) for j in (2, 1, 3)]


def from_behind(array, axis, by):
    count = lax.axis_size(axis)
    pairs = [(i, i + by) for i in range(count) if 0 <= i + by < count]
    return lax.ppermute(array, axis, pairs)


def wide(array):
    return array.astype(jnp.float32)


def call(kernel, out_shape, operands, scalars=(), after=(), scratch=(), aliases=None):
    vmem = pl.BlockSpec(memory_space=pltpu.VMEM)
    anywhere = pl.BlockSpec(memory_space=pl.ANY)
    first, last = len(scalars) + len(operands), len(scalars) + len(operands) + len(after)

    def run(*refs):
        kernel(*refs[:first], *refs[last:])

    return pl.pallas_call(
        run,
        in_specs=[pl.BlockSpec(memory_space=pltpu.SMEM)] * len(scalars)
        + [vmem] * len(operands)
        + [anywhere] * len(after),
        out_specs=[vmem] * len(out_shape),
        out_shape=[jax.ShapeDtypeStruct(shape, dtype) for shape, dtype in out_shape],
        input_output_aliases=aliases or {},
        scratch_shapes=list(scratch),
        compiler_params=pltpu.CompilerParams(vmem_limit_bytes=VMEM),
        cost_estimate=pl.CostEstimate(flops=1024, bytes_accessed=1024, transcendentals=0),
    )(*scalars, *operands, *after)


def gated(arrays, after):
    anywhere = pl.BlockSpec(memory_space=pl.ANY)
    return pl.pallas_call(
        lambda *refs: None,
        in_specs=[anywhere] * (len(arrays) + len(after)),
        out_specs=[anywhere] * len(arrays),
        out_shape=[jax.ShapeDtypeStruct(array.shape, array.dtype) for array in arrays],
        input_output_aliases={i: i for i in range(len(arrays))},
        compiler_params=pltpu.CompilerParams(vmem_limit_bytes=GATE),
        cost_estimate=pl.CostEstimate(flops=1024, bytes_accessed=1024, transcendentals=0),
    )(*arrays, *after)


class Mover:
    def __init__(self, moves, pieces, rows, cols, held, theirs):
        position = lax.axis_index("frame")
        self.y, self.x = position // (2 * SIDE), (position // 2) % SIDE
        core = position % 2
        self.core = 1 - core if theirs else core
        self.down, right = moves[0], moves[1]
        self.over = jnp.where(right < 0, 1, 0)
        self.turn = jnp.where(right < 0, LANES + right, right)
        self.rows, self.held, self.pieces = rows, held, []
        base = 0
        for source, origin, first, width in pieces:
            begin, end = max(first - LANES, 0), min(first + width + LANES, cols)
            blank = jnp.zeros(held.shape[2:], held.dtype)
            for slot in range(held.shape[0]):
                if begin == first:
                    held[slot, base] = blank
                if end == first + width:
                    held[slot, base + width // LANES + 1] = blank
            low = base + (1 if begin == first else 0)
            self.pieces.append((source, begin - origin, (end - begin) // LANES, base, low, width))
            base += width // LANES + 2

    def band(self, slot, j, d, write):
        by_x = jnp.where(self.core == 0, j, d)
        by_y = jnp.where(self.core == 0, d, j)
        chip = lax.rem(self.y + by_y, SIDE) * SIDE + lax.rem(self.x + by_x, SIDE)
        top = pl.multiple_of((chip * 2 + self.core) * BAND, BAND)
        above = pl.multiple_of(jnp.maximum(top - HALO, 0), HALO)
        below = pl.multiple_of(jnp.minimum(top + BAND, self.rows - HALO), HALO)
        has_above = jnp.where(top > 0, 1.0, 0.0).astype(jnp.float32)
        has_below = jnp.where(top + BAND < self.rows, 1.0, 0.0).astype(jnp.float32)
        lane = lax.broadcasted_iota(jnp.int32, (BAND, LANES), 1)
        held, out = self.held, 0
        for source, begin, tiles, base, low, width in self.pieces:
            for k in range(tiles):
                at = pl.ds(begin + k * LANES, LANES)
                held[slot, low + k, :PAD] = wide(source[pl.ds(above, HALO), at])[PAD:] * has_above
                held[slot, low + k, PAD : PAD + BAND] = wide(source[pl.ds(top, BAND), at])
                held[slot, low + k, PAD + BAND :] = (
                    wide(source[pl.ds(below, HALO), at])[:PAD] * has_below
                )
            before = None
            for k in range(width // LANES + 1):
                value = held[slot, base + k + self.over, pl.ds(PAD - self.down, BAND), :]
                now = pltpu.roll(value, self.turn, 1)
                if k > 0:
                    write(out, jnp.where(lane < self.turn, before, now))
                    out += LANES
                before = now


def held_for(widths):
    tiles = sum(width // LANES + 2 for width in widths)
    return pltpu.VMEM((2 if tiles > 16 else SIDE, tiles, BAND + 2 * PAD, LANES), jnp.float32)


def each_band(mover, count, where, write):
    slots = mover.held.shape[0]

    @pl.loop(0, count // slots)
    def _(turn):
        for slot in range(slots):
            n = slots * turn + slot
            j, d = where(n)
            mover.band(slot, j, d, functools.partial(write, n))


def forward(n):
    return 1 + n // 2, n


def backward(n):
    return 2 + n // 2, n


def own(n):
    return 0, n


def both_ways(n):
    return jnp.where(n < 4, forward(n)[0], backward(n - 4)[0]), lax.rem(n, SIDE)


def passing(n):
    return jnp.where(n < 2, 1, 3), lax.rem(n + 2, SIDE)


def later(n):
    return jnp.where(n < 4, passing(n)[0], 0), lax.rem(jnp.where(n < 4, n + 2, n), SIDE)


def every(n):
    return n // SIDE, lax.rem(n, SIDE)


class Columns:
    def __init__(self, moves, rows, cols, arrays, places):
        self.moves, self.rows, self.cols, self.arrays, self.places = moves, rows, cols, arrays, places
        self.total = sum(width for _, _, width in places)
        self.scratch = [held_for([width for _, _, width in places])]

    def mover(self, moves, sources, held, theirs):
        pieces = [(source, *place) for source, place in zip(sources, self.places)]
        return Mover(moves, pieces, self.rows, self.cols, held, theirs)

    def run(self, body, out_shape, operands, after=(), theirs=False):
        count = len(self.arrays)

        def kernel(moves, *refs):
            mover = self.mover(moves, [refs[0]] * len(self.places), refs[-1], theirs)
            body(mover, *refs[count:-1])

        return call(
            kernel,
            out_shape,
            [*self.arrays, *operands],
            [self.moves],
            after,
            self.scratch,
        )

    def theirs(self, count, where, after=()):
        def body(mover, out):
            def write(n, begin, value):
                out[n, :, begin : begin + LANES] = value.astype(jnp.bfloat16)

            each_band(mover, count, where, write)

        shape = ((count, BAND, self.total), jnp.bfloat16)
        return self.run(body, [shape], [], after, True)[0]

    def loaded(self, frame, low, high, middle):
        rows, cols = frame.shape
        first, last = middle[0][0], middle[-1][1]
        ends = [min(end + LANES, high) for _, end in middle]
        parts = [(0, low), (high, cols), *zip([low, *ends[:-1]], ends)]
        halves = [slice(i * rows // SIDE, (i + 1) * rows // SIDE) for i in range(SIDE)]

        def kernel(moves_far, frame, out, bands, both, held, held_middle, moves, sems, moves_sem):
            copies = [
                [
                    pltpu.make_async_copy(
                        frame.at[half, begin:end], out.at[half, begin:end], sems.at[p, h]
                    )
                    for h, half in enumerate(halves)
                ]
                for p, (begin, end) in enumerate(parts)
            ]
            moves_copy = pltpu.make_async_copy(moves_far, moves, moves_sem)
            moves_copy.start()
            for pair in copies:
                for copy in pair:
                    copy.start()
            moves_copy.wait()
            for copy in (*copies[0], *copies[1]):
                copy.wait()
            mover = self.mover(moves, [out] * len(self.places), held, True)

            def write(n, begin, value):
                bands[n, :, begin : begin + LANES] = value.astype(jnp.bfloat16)

            each_band(mover, SIDE * SIDE, every, write)
            for p, (pair, (begin, end)) in enumerate(zip(copies[2:], middle)):
                for copy in pair:
                    copy.wait()
                if p == len(middle) - 1:
                    break
                mover = Mover(moves, [(out, 0, begin, end - begin)], rows, cols, held_middle, True)

                def write_middle(n, at, value, begin=begin):
                    at = at + begin - first
                    both[n, :, at : at + LANES] = value.astype(jnp.bfloat16)

                each_band(mover, 2 * SIDE, both_ways, write_middle)

        vmem = pl.BlockSpec(memory_space=pltpu.VMEM)
        far = pl.BlockSpec(memory_space=pltpu.HBM)
        widest = max(end - begin for begin, end in middle[:-1])
        return pl.pallas_call(
            kernel,
            in_specs=[far, far],
            out_specs=[vmem, vmem, vmem],
            out_shape=[
                jax.ShapeDtypeStruct(frame.shape, frame.dtype),
                jax.ShapeDtypeStruct((SIDE * SIDE, BAND, self.total), jnp.bfloat16),
                jax.ShapeDtypeStruct((2 * SIDE, BAND, last - first), jnp.bfloat16),
            ],
            scratch_shapes=[
                *self.scratch,
                held_for([widest]),
                pltpu.SMEM(self.moves.shape, jnp.int32),
                pltpu.SemaphoreType.DMA((len(parts), len(halves))),
                pltpu.SemaphoreType.DMA,
            ],
            compiler_params=pltpu.CompilerParams(vmem_limit_bytes=LOADING),
            cost_estimate=pl.CostEstimate(flops=1024, bytes_accessed=1024, transcendentals=0),
        )(self.moves, frame)

    def theirs_rest(self, both, last, after=()):
        first = both.shape[2] - last.total

        def kernel(moves, frame, both, bands, out, held, held_last):
            mover = last.mover(moves, [frame], held_last, True)

            def write_last(n, begin, value):
                at = slice(first + begin, first + begin + LANES)
                out[n, :, at] = value.astype(jnp.bfloat16)

            each_band(mover, 2 * SIDE, both_ways, write_last)
            mover = self.mover(moves, [frame], held, True)

            def write(n, begin, value):
                bands[n, :, begin : begin + LANES] = value.astype(jnp.bfloat16)

            each_band(mover, 2 * SIDE, later, write)

        shape = ((2 * SIDE, BAND, self.total), jnp.bfloat16)
        return call(
            kernel,
            [shape, shape],
            [*self.arrays, both],
            [self.moves],
            after,
            [*self.scratch, *last.scratch],
            {2: 1},
        )

    def pairs(self, other, after=()):
        def body(mover, other, *outs):
            for way, where in enumerate((forward, backward)):

                def write(n, begin, value, way=way):
                    at = slice(begin, begin + LANES)
                    value = value + wide(other[way * SIDE + n, :, at])
                    outs[way][n, :, at] = value.astype(jnp.bfloat16)

                each_band(mover, SIDE, where, write)

        shape = ((SIDE, BAND, self.total), jnp.bfloat16)
        return self.run(body, [shape, shape], [other], after)

    def every_pair(self, other, after=()):
        def body(mover, other, *outs):
            for j in range(SIDE):

                def write(n, begin, value, j=j):
                    at = slice(begin, begin + LANES)
                    value = value + wide(other[j * SIDE + n, :, at])
                    outs[j][n, :, at] = value.astype(outs[j].dtype)

                each_band(mover, SIDE, lambda n, j=j: (j, n), write)

        quarter = (SIDE, BAND, self.total)
        shapes = [(quarter, jnp.float32)] + [(quarter, jnp.bfloat16)] * (SIDE - 1)
        return self.run(body, shapes, [other], after)

    def later_pairs(self, other, after=()):
        def body(mover, other, *outs):
            for part, out in enumerate(outs):

                def write(n, begin, value, part=part, out=out):
                    at = slice(begin, begin + LANES)
                    out[n, :, at] = value + wide(other[part * SIDE + n, :, at])

                where = (passing, own)[part]
                each_band(mover, SIDE, where, write)

        shape = ((SIDE, BAND, self.total), jnp.float32)
        return self.run(body, [shape, shape], [other], after)


def pass_kernel(pair, forth, back, out_forth, out_back):
    half = SIDE // 2
    for n in range(half):
        out_forth[n] = (pair[n] + wide(forth[half + n])).astype(out_forth.dtype)
        out_back[n] = (pair[half + n] + wide(back[n])).astype(out_back.dtype)


def chip_kernel(pair, forth, back, forth_far, back_far, *refs):
    score_refs, outs = refs[:SIDE], refs[SIDE:]
    total = pair.shape[2]
    for n in range(SIDE):
        near = forth if n < 2 else back
        far = back_far if n < 2 else forth_far
        value = pair[n] + (wide(near[n]) + wide(far[n % 2]))
        outs[n][:, :total] = value.astype(outs[n].dtype)
    score = (score_refs[0][...] + score_refs[1][...]) + (score_refs[2][...] + score_refs[3][...])
    high = wide(score.astype(jnp.bfloat16))
    middle = wide((score - high).astype(jnp.bfloat16))
    low = (score - high) - middle
    line = lax.broadcasted_iota(jnp.int32, score.shape, 0)
    three = jnp.where(line == 0, high, jnp.where(line == 1, middle, low))
    three = jnp.where(line < 3, three, 0.0)
    three = jnp.concatenate([three, jnp.zeros((BAND - PAD, LANES), jnp.float32)], 0)
    for out in outs:
        out[:, total:] = three.astype(out.dtype)


def row_kernel(mine, a, b, c, *outs):
    for d in range(SIDE):
        value = mine[d] + ((wide(a[d]) + wide(b[d])) + wide(c[d]))
        outs[d][...] = value.astype(outs[d].dtype)


def edge_kernel(scale, mine, a, b, c, left, right, right_sent):
    value = mine[...] + ((wide(a[...]) + wide(b[...])) + wide(c[...]))
    value = value * scale
    left[...] = value[:, :EDGE]
    right[...] = value[:, EDGE:]
    right_sent[...] = value[:, EDGE:].astype(jnp.bfloat16)


def rounded(ref):
    return wide(ref[...].astype(jnp.bfloat16))


def right_blend(width, shift, own_right, next_left):
    mine, after = rounded(own_right), rounded(next_left)
    column = lax.broadcasted_iota(jnp.int32, mine.shape, 1)
    aligned = pltpu.roll(after, lax.rem(STRIP - width - shift + EDGE, EDGE), 1)[:, :STRIP]
    feather = (wide(STRIP - column) - 0.5) / wide(jnp.maximum(width, 1))
    blend = feather * mine + (1.0 - feather) * aligned
    return jnp.where(column >= STRIP - width, blend, mine)


def left_blend(width, shift, own_left, prev_right):
    mine = rounded(own_left)
    rows = mine.shape[0]
    before = jnp.concatenate([rounded(prev_right), jnp.zeros((rows, LAGS), jnp.float32)], 1)
    before = pltpu.roll(before, lax.rem(shift + width - STRIP + EDGE, EDGE), 1)
    column = lax.broadcasted_iota(jnp.int32, mine.shape, 1)
    feather = (wide(width - column + shift) - 0.5) / wide(jnp.maximum(width, 1))
    blend = feather * before + (1.0 - feather) * mine
    return jnp.where((column >= shift) & (column < shift + width), blend, mine)


def blend_kernel(widths, shifts, own_left, own_right, next_left, prev_right, left, right):
    tile = lax.axis_index("tile")
    earlier = jnp.maximum(tile - 1, 0)
    value = right_blend(widths[tile], shifts[tile], own_right, next_left)
    right[...] = value.astype(jnp.bfloat16)
    width, shift = jnp.where(tile > 0, widths[earlier], 0), jnp.where(tile > 0, shifts[earlier], 0)
    left[...] = left_blend(width, shift, own_left, prev_right).astype(jnp.bfloat16)


def image_kernel(scale, left, right, mine, a, b, c, out, score):
    total = mine.shape[1] - LANES
    for begin in range(0, total, LANES):
        at = slice(begin, begin + LANES)
        value = mine[:, at] + ((wide(a[:, at]) + wide(b[:, at])) + wide(c[:, at]))
        out[:, EDGE + begin : EDGE + begin + LANES] = (value * scale).astype(jnp.bfloat16)
    out[:, :EDGE] = left[...]
    out[:, EDGE + total :] = right[...]
    at = slice(total, total + LANES)
    value = mine[:PAD, at] + ((wide(a[:, at]) + wide(b[:, at])) + wide(c[:, at]))[:PAD]
    score[...] = jnp.sum(value, axis=0, keepdims=True)


def score_kernel(all_rows, widths, own_right, next_left, score_out):
    width = widths[lax.axis_index("tile")]
    column = lax.broadcasted_iota(jnp.int32, own_right.shape, 1)
    masked = jnp.where(column >= STRIP - width, own_right[...], 0.0)
    masked = pltpu.roll(masked, lax.rem(width, STRIP), 1)
    after = next_left[...]
    mine_high, after_high = masked.astype(jnp.bfloat16), after.astype(jnp.bfloat16)
    mine_low = (masked - wide(mine_high)).astype(jnp.bfloat16)
    after_low = (after - wide(after_high)).astype(jnp.bfloat16)
    pairs = ((mine_high, after_high), (mine_high, after_low), (mine_low, after_high))
    starts = range(0, STRIP, LANES)
    gram = lax.dot_general(
        jnp.concatenate([one[:, t : t + LANES] for one, _ in pairs for t in starts], 0),
        jnp.concatenate([two[:, t : t + 2 * LANES] for _, two in pairs for t in starts], 0),
        (((0,), (0,)), ((), ())),
        preferred_element_type=jnp.float32,
    )
    line = lax.broadcasted_iota(jnp.int32, gram.shape, 0)
    step = 1
    while step < LANES:
        gram = jnp.where((line & step) != 0, pltpu.roll(gram, 2 * LANES - step, 1), gram)
        step *= 2
    total = jnp.sum(gram[:, :LANES], axis=0, keepdims=True)
    terms = jnp.full((PAD, LANES), all_rows * jnp.maximum(width, 1), jnp.int32)
    score_out[...] = jnp.broadcast_to(total, (PAD, LANES)) / jnp.sqrt(terms.astype(jnp.float32))


def body(movie, frame_shift, intersection, seam_shift):
    frame = movie[0, 0]
    rows, cols = frame.shape
    scale = 1.0 / math.sqrt(lax.axis_size("frame"))
    moves = frame_shift[0, 0]

    low, high = EDGE + LANES, cols - STRIP - LANES
    places = [(0, 0, EDGE), (0, cols - STRIP, STRIP)]
    ninth = (cols - STRIP - EDGE) // 9 // LANES * LANES
    cuts = [EDGE, EDGE + 4 * ninth, EDGE + 7 * ninth, cols - STRIP]
    frame, theirs_s, theirs_m = Columns(moves, rows, cols, [], places).loaded(
        frame, low, high, list(zip(cuts[:-1], cuts[1:]))
    )
    strips = Columns(moves, rows, cols, [frame], places)
    middle = Columns(moves, rows, cols, [frame], [(0, EDGE, cols - STRIP - EDGE)])

    other_s = to_other_core(theirs_s)
    ending = Columns(moves, rows, cols, [frame], [(0, cuts[-2], cuts[-1] - cuts[-2])])
    theirs_l, theirs_m = middle.theirs_rest(theirs_m, ending, [theirs_s])
    other_m = to_other_core(*gated([theirs_m], [other_s]))
    other_l = to_other_core(theirs_l)
    pair_s = strips.every_pair(other_s, [theirs_l])
    got_s = direct(pair_s, 1)
    pair_m = middle.pairs(other_m, [pair_s[0]])
    pair_f, pair_b = gated(pair_m, got_s)
    got_f, got_b = ahead(pair_f, 1, 1), ahead(pair_b, 1, -1)

    band = (BAND, EDGE + STRIP)
    row_s = call(
        row_kernel,
        [(band, jnp.float32)] + [(band, jnp.bfloat16)] * (SIDE - 1),
        [pair_s[0], *got_s],
        after=[pair_f, other_l],
    )
    own_left, own_right, sent_right = call(
        functools.partial(edge_kernel, scale),
        [((BAND, EDGE), jnp.float32), ((BAND, STRIP), jnp.float32), ((BAND, STRIP), jnp.bfloat16)],
        [row_s[0], *direct(row_s, 2)],
    )
    next_left = from_behind(own_left, "tile", -1)
    prev_right = from_behind(sent_right, "tile", 1)
    passing_m, own_m = middle.later_pairs(other_l, [own_left])
    (score,) = call(
        functools.partial(score_kernel, rows),
        [((PAD, LANES), jnp.float32)],
        [own_right, next_left],
        [intersection],
        after=[passing_m],
    )

    half = (SIDE // 2, BAND, middle.total)
    far_f, far_b = call(
        pass_kernel,
        [(half, jnp.bfloat16)] * 2,
        [passing_m, got_f, got_b],
        after=[score],
    )
    far_f, far_b = ahead(far_f, 1, 1), ahead(far_b, 1, -1)
    score = score + to_other_core(score)
    wider = (BAND, middle.total + LANES)
    row_m = call(
        chip_kernel,
        [(wider, jnp.float32)] + [(wider, jnp.bfloat16)] * (SIDE - 1),
        [own_m, got_f, got_b, far_f, far_b, *[score], *direct([score] * SIDE, 1)],
    )
    left_part, right_part = call(
        blend_kernel,
        [((BAND, EDGE), jnp.bfloat16), ((BAND, STRIP), jnp.bfloat16)],
        [own_left, own_right, next_left, prev_right],
        [intersection, seam_shift],
    )
    image, score = call(
        functools.partial(image_kernel, scale),
        [((BAND, cols), jnp.bfloat16), ((1, LAGS), jnp.float32)],
        [left_part, right_part, row_m[0], *direct(row_m, 2)],
    )
    return (image[None], score)


def solution(mesh):
    placed = (P("tile", "frame", None, None), P("tile", "frame", None), P(), P())
    return jax.shard_map(
        body,
        mesh=mesh,
        in_specs=placed,
        out_specs=(P("tile", "frame", None), P("tile", None)),
        check_vma=False,
    )
```

```python
import functools
import math

import jax
import jax.numpy as jnp
from jax import lax
from jax.experimental import pallas as pl
from jax.experimental.pallas import tpu as pltpu
from jax.sharding import PartitionSpec as P

STRIP = 512
LAGS = 128
LANES = 128
EDGE = STRIP + LAGS
SIDE = 4
BAND = 32
HALO = 16
PAD = 8
VMEM = 16 * 1024 * 1024
GATE = 1024 * 1024
LOADING = 36 * 1024 * 1024


def device_at(y, x, core):
    return (y * SIDE + x) * 2 + core


def permuted(array, target):
    places = [(y, x, core) for y in range(SIDE) for x in range(SIDE) for core in range(2)]
    return lax.ppermute(
        array, "frame", [(device_at(*place), device_at(*target(*place))) for place in places]
    )


def to_other_core(array):
    return permuted(array, lambda y, x, core: (y, x, 1 - core))


def ahead(array, stage, by):
    def target(y, x, core):
        if (core == 0) == (stage == 1):
            return (y, (x + by) % SIDE, core)
        return ((y + by) % SIDE, x, core)

    return permuted(array, target)


def direct(arrays, stage):
    return [ahead(arrays[j], stage, j) for j in (2, 1, 3)]


def from_behind(array, axis, by):
    count = lax.axis_size(axis)
    pairs = [(i, i + by) for i in range(count) if 0 <= i + by < count]
    return lax.ppermute(array, axis, pairs)


def wide(array):
    return array.astype(jnp.float32)


def call(kernel, out_shape, operands, scalars=(), after=(), scratch=(), aliases=None):
    vmem = pl.BlockSpec(memory_space=pltpu.VMEM)
    anywhere = pl.BlockSpec(memory_space=pl.ANY)
    first, last = len(scalars) + len(operands), len(scalars) + len(operands) + len(after)

    def run(*refs):
        kernel(*refs[:first], *refs[last:])

    return pl.pallas_call(
        run,
        in_specs=[pl.BlockSpec(memory_space=pltpu.SMEM)] * len(scalars)
        + [vmem] * len(operands)
        + [anywhere] * len(after),
        out_specs=[vmem] * len(out_shape),
        out_shape=[jax.ShapeDtypeStruct(shape, dtype) for shape, dtype in out_shape],
        input_output_aliases=aliases or {},
        scratch_shapes=list(scratch),
        compiler_params=pltpu.CompilerParams(vmem_limit_bytes=VMEM),
        cost_estimate=pl.CostEstimate(flops=1024, bytes_accessed=1024, transcendentals=0),
    )(*scalars, *operands, *after)


def gated(arrays, after):
    anywhere = pl.BlockSpec(memory_space=pl.ANY)
    return pl.pallas_call(
        lambda *refs: None,
        in_specs=[anywhere] * (len(arrays) + len(after)),
        out_specs=[anywhere] * len(arrays),
        out_shape=[jax.ShapeDtypeStruct(array.shape, array.dtype) for array in arrays],
        input_output_aliases={i: i for i in range(len(arrays))},
        compiler_params=pltpu.CompilerParams(vmem_limit_bytes=GATE),
        cost_estimate=pl.CostEstimate(flops=1024, bytes_accessed=1024, transcendentals=0),
    )(*arrays, *after)


class Mover:
    def __init__(self, moves, pieces, rows, cols, held, theirs):
        position = lax.axis_index("frame")
        self.y, self.x = position // (2 * SIDE), (position // 2) % SIDE
        core = position % 2
        self.core = 1 - core if theirs else core
        self.down, right = moves[0], moves[1]
        self.over = jnp.where(right < 0, 1, 0)
        self.turn = jnp.where(right < 0, LANES + right, right)
        self.rows, self.held, self.pieces = rows, held, []
        base = 0
        for source, origin, first, width in pieces:
            begin, end = max(first - LANES, 0), min(first + width + LANES, cols)
            blank = jnp.zeros(held.shape[2:], held.dtype)
            for slot in range(held.shape[0]):
                if begin == first:
                    held[slot, base] = blank
                if end == first + width:
                    held[slot, base + width // LANES + 1] = blank
            low = base + (1 if begin == first else 0)
            self.pieces.append((source, begin - origin, (end - begin) // LANES, base, low, width))
            base += width // LANES + 2

    def band(self, slot, j, d, write):
        by_x = jnp.where(self.core == 0, j, d)
        by_y = jnp.where(self.core == 0, d, j)
        chip = lax.rem(self.y + by_y, SIDE) * SIDE + lax.rem(self.x + by_x, SIDE)
        top = pl.multiple_of((chip * 2 + self.core) * BAND, BAND)
        above = pl.multiple_of(jnp.maximum(top - HALO, 0), HALO)
        below = pl.multiple_of(jnp.minimum(top + BAND, self.rows - HALO), HALO)
        has_above = jnp.where(top > 0, 1.0, 0.0).astype(jnp.float32)
        has_below = jnp.where(top + BAND < self.rows, 1.0, 0.0).astype(jnp.float32)
        lane = lax.broadcasted_iota(jnp.int32, (BAND, LANES), 1)
        held, out = self.held, 0
        for source, begin, tiles, base, low, width in self.pieces:
            for k in range(tiles):
                at = pl.ds(begin + k * LANES, LANES)
                held[slot, low + k, :PAD] = wide(source[pl.ds(above, HALO), at])[PAD:] * has_above
                held[slot, low + k, PAD : PAD + BAND] = wide(source[pl.ds(top, BAND), at])
                held[slot, low + k, PAD + BAND :] = (
                    wide(source[pl.ds(below, HALO), at])[:PAD] * has_below
                )
            before = None
            for k in range(width // LANES + 1):
                value = held[slot, base + k + self.over, pl.ds(PAD - self.down, BAND), :]
                now = pltpu.roll(value, self.turn, 1)
                if k > 0:
                    write(out, jnp.where(lane < self.turn, before, now))
                    out += LANES
                before = now


def held_for(widths):
    tiles = sum(width // LANES + 2 for width in widths)
    return pltpu.VMEM((2 if tiles > 16 else SIDE, tiles, BAND + 2 * PAD, LANES), jnp.float32)


def each_band(mover, count, where, write):
    slots = mover.held.shape[0]

    @pl.loop(0, count // slots)
    def _(turn):
        for slot in range(slots):
            n = slots * turn + slot
            j, d = where(n)
            mover.band(slot, j, d, functools.partial(write, n))


def forward(n):
    return 1 + n // 2, n


def backward(n):
    return 2 + n // 2, n


def own(n):
    return 0, n


def both_ways(n):
    return jnp.where(n < 4, forward(n)[0], backward(n - 4)[0]), lax.rem(n, SIDE)


def passing(n):
    return jnp.where(n < 2, 1, 3), lax.rem(n + 2, SIDE)


def later(n):
    return jnp.where(n < 4, passing(n)[0], 0), lax.rem(jnp.where(n < 4, n + 2, n), SIDE)


def every(n):
    return n // SIDE, lax.rem(n, SIDE)


class Columns:
    def __init__(self, moves, rows, cols, arrays, places):
        self.moves, self.rows, self.cols, self.arrays, self.places = moves, rows, cols, arrays, places
        self.total = sum(width for _, _, width in places)
        self.scratch = [held_for([width for _, _, width in places])]

    def mover(self, moves, sources, held, theirs):
        pieces = [(source, *place) for source, place in zip(sources, self.places)]
        return Mover(moves, pieces, self.rows, self.cols, held, theirs)

    def run(self, body, out_shape, operands, after=(), theirs=False):
        count = len(self.arrays)

        def kernel(moves, *refs):
            mover = self.mover(moves, [refs[0]] * len(self.places), refs[-1], theirs)
            body(mover, *refs[count:-1])

        return call(
            kernel,
            out_shape,
            [*self.arrays, *operands],
            [self.moves],
            after,
            self.scratch,
        )

    def theirs(self, count, where, after=()):
        def body(mover, out):
            def write(n, begin, value):
                out[n, :, begin : begin + LANES] = value.astype(jnp.bfloat16)

            each_band(mover, count, where, write)

        shape = ((count, BAND, self.total), jnp.bfloat16)
        return self.run(body, [shape], [], after, True)[0]

    def loaded(self, frame, low, high, middle):
        rows, cols = frame.shape
        first, last = middle[0][0], middle[-1][1]
        ends = [min(end + LANES, high) for _, end in middle]
        parts = [(0, low), (high, cols), *zip([low, *ends[:-1]], ends)]
        halves = [slice(i * rows // SIDE, (i + 1) * rows // SIDE) for i in range(SIDE)]

        def kernel(moves_far, frame, out, bands, both, held, held_middle, moves, sems, moves_sem):
            copies = [
                [
                    pltpu.make_async_copy(
                        frame.at[half, begin:end], out.at[half, begin:end], sems.at[p, h]
                    )
                    for h, half in enumerate(halves)
                ]
                for p, (begin, end) in enumerate(parts)
            ]
            moves_copy = pltpu.make_async_copy(moves_far, moves, moves_sem)
            moves_copy.start()
            for pair in copies:
                for copy in pair:
                    copy.start()
            moves_copy.wait()
            for copy in (*copies[0], *copies[1]):
                copy.wait()
            mover = self.mover(moves, [out] * len(self.places), held, True)

            def write(n, begin, value):
                bands[n, :, begin : begin + LANES] = value.astype(jnp.bfloat16)

            each_band(mover, SIDE * SIDE, every, write)
            for p, (pair, (begin, end)) in enumerate(zip(copies[2:], middle)):
                for copy in pair:
                    copy.wait()
                if p == len(middle) - 1:
                    break
                mover = Mover(moves, [(out, 0, begin, end - begin)], rows, cols, held_middle, True)

                def write_middle(n, at, value, begin=begin):
                    at = at + begin - first
                    both[n, :, at : at + LANES] = value.astype(jnp.bfloat16)

                each_band(mover, 2 * SIDE, both_ways, write_middle)

        vmem = pl.BlockSpec(memory_space=pltpu.VMEM)
        far = pl.BlockSpec(memory_space=pltpu.HBM)
        widest = max(end - begin for begin, end in middle[:-1])
        return pl.pallas_call(
            kernel,
            in_specs=[far, far],
            out_specs=[vmem, vmem, vmem],
            out_shape=[
                jax.ShapeDtypeStruct(frame.shape, frame.dtype),
                jax.ShapeDtypeStruct((SIDE * SIDE, BAND, self.total), jnp.bfloat16),
                jax.ShapeDtypeStruct((2 * SIDE, BAND, last - first), jnp.bfloat16),
            ],
            scratch_shapes=[
                *self.scratch,
                held_for([widest]),
                pltpu.SMEM(self.moves.shape, jnp.int32),
                pltpu.SemaphoreType.DMA((len(parts), len(halves))),
                pltpu.SemaphoreType.DMA,
            ],
            compiler_params=pltpu.CompilerParams(vmem_limit_bytes=LOADING),
            cost_estimate=pl.CostEstimate(flops=1024, bytes_accessed=1024, transcendentals=0),
        )(self.moves, frame)

    def theirs_rest(self, both, last, after=()):
        first = both.shape[2] - last.total

        def kernel(moves, frame, both, bands, out, held, held_last):
            mover = last.mover(moves, [frame], held_last, True)

            def write_last(n, begin, value):
                at = slice(first + begin, first + begin + LANES)
                out[n, :, at] = value.astype(jnp.bfloat16)

            each_band(mover, 2 * SIDE, both_ways, write_last)
            mover = self.mover(moves, [frame], held, True)

            def write(n, begin, value):
                bands[n, :, begin : begin + LANES] = value.astype(jnp.bfloat16)

            each_band(mover, 2 * SIDE, later, write)

        shape = ((2 * SIDE, BAND, self.total), jnp.bfloat16)
        return call(
            kernel,
            [shape, shape],
            [*self.arrays, both],
            [self.moves],
            after,
            [*self.scratch, *last.scratch],
            {2: 1},
        )

    def pairs(self, other, after=()):
        def body(mover, other, *outs):
            for way, where in enumerate((forward, backward)):

                def write(n, begin, value, way=way):
                    at = slice(begin, begin + LANES)
                    value = value + wide(other[way * SIDE + n, :, at])
                    outs[way][n, :, at] = value.astype(jnp.bfloat16)

                each_band(mover, SIDE, where, write)

        shape = ((SIDE, BAND, self.total), jnp.bfloat16)
        return self.run(body, [shape, shape], [other], after)

    def every_pair(self, other, after=()):
        def body(mover, other, *outs):
            for j in range(SIDE):

                def write(n, begin, value, j=j):
                    at = slice(begin, begin + LANES)
                    value = value + wide(other[j * SIDE + n, :, at])
                    outs[j][n, :, at] = value.astype(outs[j].dtype)

                each_band(mover, SIDE, lambda n, j=j: (j, n), write)

        quarter = (SIDE, BAND, self.total)
        shapes = [(quarter, jnp.float32)] + [(quarter, jnp.bfloat16)] * (SIDE - 1)
        return self.run(body, shapes, [other], after)

    def later_pairs(self, other, after=()):
        def body(mover, other, *outs):
            for part, out in enumerate(outs):

                def write(n, begin, value, part=part, out=out):
                    at = slice(begin, begin + LANES)
                    out[n, :, at] = value + wide(other[part * SIDE + n, :, at])

                where = (passing, own)[part]
                each_band(mover, SIDE, where, write)

        shape = ((SIDE, BAND, self.total), jnp.float32)
        return self.run(body, [shape, shape], [other], after)


def pass_kernel(pair, forth, back, out_forth, out_back):
    half = SIDE // 2
    for n in range(half):
        out_forth[n] = (pair[n] + wide(forth[half + n])).astype(out_forth.dtype)
        out_back[n] = (pair[half + n] + wide(back[n])).astype(out_back.dtype)


def chip_kernel(pair, forth, back, forth_far, back_far, *refs):
    score_refs, outs = refs[:SIDE], refs[SIDE:]
    total = pair.shape[2]
    for n in range(SIDE):
        near = forth if n < 2 else back
        far = back_far if n < 2 else forth_far
        value = pair[n] + (wide(near[n]) + wide(far[n % 2]))
        outs[n][:, :total] = value.astype(outs[n].dtype)
    score = (score_refs[0][...] + score_refs[1][...]) + (score_refs[2][...] + score_refs[3][...])
    high = wide(score.astype(jnp.bfloat16))
    middle = wide((score - high).astype(jnp.bfloat16))
    low = (score - high) - middle
    line = lax.broadcasted_iota(jnp.int32, score.shape, 0)
    three = jnp.where(line == 0, high, jnp.where(line == 1, middle, low))
    three = jnp.where(line < 3, three, 0.0)
    three = jnp.concatenate([three, jnp.zeros((BAND - PAD, LANES), jnp.float32)], 0)
    for out in outs:
        out[:, total:] = three.astype(out.dtype)


def row_kernel(mine, a, b, c, *outs):
    for d in range(SIDE):
        value = mine[d] + ((wide(a[d]) + wide(b[d])) + wide(c[d]))
        outs[d][...] = value.astype(outs[d].dtype)


def edge_kernel(scale, mine, a, b, c, left, right, right_sent):
    value = mine[...] + ((wide(a[...]) + wide(b[...])) + wide(c[...]))
    value = value * scale
    left[...] = value[:, :EDGE]
    right[...] = value[:, EDGE:]
    right_sent[...] = value[:, EDGE:].astype(jnp.bfloat16)


def rounded(ref):
    return wide(ref[...].astype(jnp.bfloat16))


def right_blend(width, shift, own_right, next_left):
    mine, after = rounded(own_right), rounded(next_left)
    column = lax.broadcasted_iota(jnp.int32, mine.shape, 1)
    aligned = pltpu.roll(after, lax.rem(STRIP - width - shift + EDGE, EDGE), 1)[:, :STRIP]
    feather = (wide(STRIP - column) - 0.5) / wide(jnp.maximum(width, 1))
    blend = feather * mine + (1.0 - feather) * aligned
    return jnp.where(column >= STRIP - width, blend, mine)


def left_blend(width, shift, own_left, prev_right):
    mine = rounded(own_left)
    rows = mine.shape[0]
    before = jnp.concatenate([rounded(prev_right), jnp.zeros((rows, LAGS), jnp.float32)], 1)
    before = pltpu.roll(before, lax.rem(shift + width - STRIP + EDGE, EDGE), 1)
    column = lax.broadcasted_iota(jnp.int32, mine.shape, 1)
    feather = (wide(width - column + shift) - 0.5) / wide(jnp.maximum(width, 1))
    blend = feather * before + (1.0 - feather) * mine
    return jnp.where((column >= shift) & (column < shift + width), blend, mine)


def blend_kernel(widths, shifts, own_left, own_right, next_left, prev_right, left, right):
    tile = lax.axis_index("tile")
    earlier = jnp.maximum(tile - 1, 0)
    value = right_blend(widths[tile], shifts[tile], own_right, next_left)
    right[...] = value.astype(jnp.bfloat16)
    width, shift = jnp.where(tile > 0, widths[earlier], 0), jnp.where(tile > 0, shifts[earlier], 0)
    left[...] = left_blend(width, shift, own_left, prev_right).astype(jnp.bfloat16)


def image_kernel(scale, left, right, mine, a, b, c, out, score):
    total = mine.shape[1] - LANES
    for begin in range(0, total, LANES):
        at = slice(begin, begin + LANES)
        value = mine[:, at] + ((wide(a[:, at]) + wide(b[:, at])) + wide(c[:, at]))
        out[:, EDGE + begin : EDGE + begin + LANES] = (value * scale).astype(jnp.bfloat16)
    out[:, :EDGE] = left[...]
    out[:, EDGE + total :] = right[...]
    at = slice(total, total + LANES)
    value = mine[:PAD, at] + ((wide(a[:, at]) + wide(b[:, at])) + wide(c[:, at]))[:PAD]
    score[...] = jnp.sum(value, axis=0, keepdims=True)


def score_kernel(all_rows, widths, own_right, next_left, score_out):
    width = widths[lax.axis_index("tile")]
    column = lax.broadcasted_iota(jnp.int32, own_right.shape, 1)
    masked = jnp.where(column >= STRIP - width, own_right[...], 0.0)
    masked = pltpu.roll(masked, lax.rem(width, STRIP), 1)
    after = next_left[...]
    mine_high, after_high = masked.astype(jnp.bfloat16), after.astype(jnp.bfloat16)
    mine_low = (masked - wide(mine_high)).astype(jnp.bfloat16)
    after_low = (after - wide(after_high)).astype(jnp.bfloat16)
    pairs = ((mine_high, after_high), (mine_high, after_low), (mine_low, after_high))
    starts = range(0, STRIP, LANES)
    gram = lax.dot_general(
        jnp.concatenate([one[:, t : t + LANES] for one, _ in pairs for t in starts], 0),
        jnp.concatenate([two[:, t : t + 2 * LANES] for _, two in pairs for t in starts], 0),
        (((0,), (0,)), ((), ())),
        preferred_element_type=jnp.float32,
    )
    line = lax.broadcasted_iota(jnp.int32, gram.shape, 0)
    step = 1
    while step < LANES:
        gram = jnp.where((line & step) != 0, pltpu.roll(gram, 2 * LANES - step, 1), gram)
        step *= 2
    total = jnp.sum(gram[:, :LANES], axis=0, keepdims=True)
    terms = jnp.full((PAD, LANES), all_rows * jnp.maximum(width, 1), jnp.int32)
    score_out[...] = jnp.broadcast_to(total, (PAD, LANES)) / jnp.sqrt(terms.astype(jnp.float32))


def body(movie, frame_shift, intersection, seam_shift):
    frame = movie[0, 0]
    rows, cols = frame.shape
    scale = 1.0 / math.sqrt(lax.axis_size("frame"))
    moves = frame_shift[0, 0]

    low, high = EDGE + LANES, cols - STRIP - LANES
    places = [(0, 0, EDGE), (0, cols - STRIP, STRIP)]
    ninth = (cols - STRIP - EDGE) // 9 // LANES * LANES
    cuts = [EDGE, EDGE + 4 * ninth, EDGE + 6 * ninth, cols - STRIP]
    frame, theirs_s, theirs_m = Columns(moves, rows, cols, [], places).loaded(
        frame, low, high, list(zip(cuts[:-1], cuts[1:]))
    )
    strips = Columns(moves, rows, cols, [frame], places)
    middle = Columns(moves, rows, cols, [frame], [(0, EDGE, cols - STRIP - EDGE)])

    other_s = to_other_core(theirs_s)
    ending = Columns(moves, rows, cols, [frame], [(0, cuts[-2], cuts[-1] - cuts[-2])])
    theirs_l, theirs_m = middle.theirs_rest(theirs_m, ending, [theirs_s])
    other_m = to_other_core(*gated([theirs_m], [other_s]))
    other_l = to_other_core(theirs_l)
    pair_s = strips.every_pair(other_s, [theirs_l])
    got_s = direct(pair_s, 1)
    pair_m = middle.pairs(other_m, [pair_s[0]])
    pair_f, pair_b = gated(pair_m, got_s)
    got_f, got_b = ahead(pair_f, 1, 1), ahead(pair_b, 1, -1)

    band = (BAND, EDGE + STRIP)
    row_s = call(
        row_kernel,
        [(band, jnp.float32)] + [(band, jnp.bfloat16)] * (SIDE - 1),
        [pair_s[0], *got_s],
        after=[pair_f, other_l],
    )
    own_left, own_right, sent_right = call(
        functools.partial(edge_kernel, scale),
        [((BAND, EDGE), jnp.float32), ((BAND, STRIP), jnp.float32), ((BAND, STRIP), jnp.bfloat16)],
        [row_s[0], *direct(row_s, 2)],
    )
    next_left = from_behind(own_left, "tile", -1)
    prev_right = from_behind(sent_right, "tile", 1)
    passing_m, own_m = middle.later_pairs(other_l, [own_left])
    (score,) = call(
        functools.partial(score_kernel, rows),
        [((PAD, LANES), jnp.float32)],
        [own_right, next_left],
        [intersection],
        after=[passing_m],
    )

    half = (SIDE // 2, BAND, middle.total)
    far_f, far_b = call(
        pass_kernel,
        [(half, jnp.bfloat16)] * 2,
        [passing_m, got_f, got_b],
        after=[score],
    )
    far_f, far_b = ahead(far_f, 1, 1), ahead(far_b, 1, -1)
    score = score + to_other_core(score)
    wider = (BAND, middle.total + LANES)
    row_m = call(
        chip_kernel,
        [(wider, jnp.float32)] + [(wider, jnp.bfloat16)] * (SIDE - 1),
        [own_m, got_f, got_b, far_f, far_b, *[score], *direct([score] * SIDE, 1)],
    )
    left_part, right_part = call(
        blend_kernel,
        [((BAND, EDGE), jnp.bfloat16), ((BAND, STRIP), jnp.bfloat16)],
        [own_left, own_right, next_left, prev_right],
        [intersection, seam_shift],
    )
    image, score = call(
        functools.partial(image_kernel, scale),
        [((BAND, cols), jnp.bfloat16), ((1, LAGS), jnp.float32)],
        [left_part, right_part, row_m[0], *direct(row_m, 2)],
    )
    return (image[None], score)


def solution(mesh):
    placed = (P("tile", "frame", None, None), P("tile", "frame", None), P(), P())
    return jax.shard_map(
        body,
        mesh=mesh,
        in_specs=placed,
        out_specs=(P("tile", "frame", None), P("tile", None)),
        check_vma=False,
    )
```
